128 devices in a mesh: ex: 16 (over z, y), bf: 8 (over x, core).
Axes of the slice: x: 4, y: 4, z: 4, core: 2. Of those that a mesh axis runs over, the one named last changes fastest.
Arguments:
- gradients: float32 [16, 16, 262144], P('ex', None, 'bf'), may hold values from -6 to 6
- moment_one: float32 [4194304], P(('ex', 'bf')), may hold values from -0.6 to 0.6
- moment_two: float32 [4194304], P(('ex', 'bf')), may hold values from 0.0025 to 0.04
- rademacher: int32 [4194304], P(('ex', 'bf')), may hold values from -1 to 1, as said below
- sample_rows: int32 [8192], replicated, may hold values from 0 to 4194303
- pool_order: int32 [16], replicated, may hold values from 0 to 15, each once
Outputs:
- sketch: float32 [16, 8192], P('ex', 'bf')
The draws below stay inside these ranges and needn't reach their ends.
Inputs may be any that keep to these rules, and one draw needn't show every extreme that they name: `rademacher`: every entry is +1 or -1, never 0. `pool_order`: each of the 16 pool numbers occurs once.
All inputs are finite; a program needn't handle non-finite values.
Results may differ from the reference program's by a relative error of at most 0.0001.
Values sent between devices are 32-bit elements; how exact they have to be, the bound alone decides.
A program may use at most 64 MiB of HBM per device.

```python
import math
import jax
import jax.numpy as jnp
from jax import lax

P_SIZE = 4194304
K = 8192
EXAMPLES = 16
N_EX = 16


def draw_rademacher(key, part):
    key = jax.random.fold_in(key, 7)
    coins = jax.random.randint(key, (P_SIZE,), 0, 2, dtype=jnp.int32)
    return 2 * coins - 1


def set_ends(drawn, rng, low, top_value):
    longest = drawn.shape.index(max(drawn.shape))
    spots = []
    for shift in (0, 1):
        where = [jax.random.randint(jax.random.fold_in(rng, axis), (), 0, length) for axis, length in enumerate(drawn.shape)]
        where[longest] = (where[longest] + shift) % drawn.shape[longest]
        spots.append(tuple(where))
    return drawn.at[spots[0]].set(low).at[spots[1]].set(top_value)


def steps_of(stream_key, extent, split, low, largest):
    level, own = 1.0, jax.random.fold_in(stream_key, 6)
    for axis_at, parts in split:
        heights = jnp.exp(jax.random.uniform(jax.random.fold_in(own, axis_at), (parts,), jnp.float32, low / len(split), largest / len(split)))
        level = level * jnp.repeat(heights, extent[axis_at] // parts).reshape([-1 if axis == axis_at else 1 for axis in range(len(extent))])
    return level


def noise(own_key, shape, scale, reach, shards=(), held_as=jnp.bfloat16):
    array = scale * jax.random.normal(own_key, shape, jnp.float32)
    if shards:
        array = array * steps_of(own_key, shape, shards, -0.22, 0.18)
    return jnp.clip(array, -reach, reach).astype(held_as)


def setup_inputs(seed: int = 0) -> dict:
    keys = jax.random.split(jax.random.key(seed), 7)
    gradients = noise(keys[0], (EXAMPLES, N_EX, P_SIZE // N_EX), 1.0, 6.0, ((0, 16), (2, 8)), jnp.float32)
    moment_one = noise(keys[1], (P_SIZE,), 0.1, 0.6, ((0, 128),), jnp.float32)
    moment_two = jnp.clip(jnp.exp(math.log(0.04) - 2.7725887 * jax.random.uniform(keys[2], (P_SIZE,), jnp.float32) ** steps_of(keys[2], (P_SIZE,), ((0, 128),), -0.2, 0.2)), 0.0025, 0.04)
    rademacher = draw_rademacher(jax.random.fold_in(keys[6], 71), 0)
    sample_rows = set_ends(jax.random.randint(keys[4], (K,), 0, P_SIZE), jax.random.fold_in(keys[4], 1), 0, P_SIZE - 1).astype(jnp.int32)
    pool_order = jax.random.permutation(keys[5], EXAMPLES).astype(jnp.int32)
    return dict(gradients=gradients, moment_one=moment_one, moment_two=moment_two, rademacher=rademacher, sample_rows=sample_rows, pool_order=pool_order)


BETA_ONE = 0.9
BETA_TWO = 0.999

def bit_parity(values, width_bits):
    counted = jnp.zeros_like(values)
    for position in range(width_bits):
        counted = counted + jnp.bitwise_and(jnp.right_shift(values, position), 1)
    return jnp.bitwise_and(counted, 1)

def hadamard_matrix(matrix_order):
    indices = jnp.arange(matrix_order, dtype=jnp.int32)
    parity = bit_parity(jnp.bitwise_and(indices[:, None], indices[None, :]), max(matrix_order.bit_length() - 1, 1))
    return (1 - 2 * parity).astype(jnp.float32)

def adam_feature(gradient, moment_one, moment_two, sign_flip):
    moment_new = BETA_ONE * moment_one + (1.0 - BETA_ONE) * gradient
    second_new = BETA_TWO * moment_two + (1.0 - BETA_TWO) * gradient * gradient
    return sign_flip * moment_new * lax.rsqrt(second_new)

def reference(gradients, moment_one, moment_two, rademacher, sample_rows, pool_order):
    param_count = moment_one.shape[0]
    total_bits = param_count.bit_length() - 1
    first_bits = total_bits // 3
    second_bits = (total_bits - first_bits) // 2
    third_bits = total_bits - first_bits - second_bits
    first_mat = hadamard_matrix(2 ** first_bits)
    second_mat = hadamard_matrix(2 ** second_bits)
    third_mat = hadamard_matrix(2 ** third_bits)
    sign_flip = rademacher.astype(jnp.float32)
    scale_out = float(param_count) ** (-0.5)

    def one_example(grad_rows):
        feature = adam_feature(grad_rows.reshape(param_count), moment_one, moment_two, sign_flip)
        volume = feature.reshape(2 ** first_bits, 2 ** second_bits, 2 ** third_bits)
        volume = jnp.einsum('abc,ad->dbc', volume, first_mat, precision=lax.Precision.HIGHEST)
        volume = jnp.einsum('abc,bd->adc', volume, second_mat, precision=lax.Precision.HIGHEST)
        volume = jnp.einsum('abc,cd->abd', volume, third_mat, precision=lax.Precision.HIGHEST)
        return jnp.take(volume.reshape(param_count), sample_rows) * scale_out
    sampled = lax.map(one_example, gradients)
    return jnp.zeros_like(sampled).at[pool_order].set(sampled)
```

```python
import functools

import jax
import jax.numpy as jnp
from jax import lax
from jax.experimental import pallas as pl
from jax.experimental.pallas import tpu as pltpu
from jax.sharding import PartitionSpec as P

MESH = pl.DeviceIdType.MESH
BETA_ONE = 0.9
BETA_TWO = 0.999
RING = 4
EX = RING * RING
BF = 2 * RING
DEPTH = 256
ROWS = 16
CHUNK = DEPTH * ROWS
TILE = 1024

STEPS = [(2, 2), (1, 1), (3, 3), (2, 0), (0, 2), (1, 3), (3, 1), (2, 1), (1, 2), (2, 3), (3, 2), (0, 1), (1, 0), (0, 3), (3, 0)]


def parity_sign(values):
    values = values ^ (values >> 4)
    values = values ^ (values >> 2)
    values = values ^ (values >> 1)
    return 1 - 2 * (values & 1)


def kernel(
    g_ref, one_ref, two_ref, flip_ref, rows_ref, pool_ref, out_ref,
    recv, one, two, flip, weight, sign_low, sign_high, high, low, part, got_core, half, got_x, mine, got_ex,
    local_sem, send_sem, recv_sem, core_sem, x_send, x_recv, ex_send, ex_recv,
):
    ex = lax.axis_index("ex")
    bf = lax.axis_index("bf")
    z, y = ex // RING, ex % RING
    x, core = bf // 2, bf % 2
    block_len = g_ref.shape[1]
    count = rows_ref.shape[1]
    chunks = block_len // CHUNK
    width = count // BF

    def owner(dz, dy):
        return (z + dz) % RING * RING + (y + dy) % RING

    def x_peer(dx):
        return (x + dx) % RING * 2 + core

    sibling = x * 2 + 1 - core

    barrier = pltpu.get_barrier_semaphore()
    for dz, dy in STEPS:
        pl.semaphore_signal(barrier, inc=1, device_id=(owner(dz, dy), bf), device_id_type=MESH)
    for dx in (1, 2, 3):
        pl.semaphore_signal(barrier, inc=1, device_id=(ex, x_peer(dx)), device_id_type=MESH)
    pl.semaphore_signal(barrier, inc=1, device_id=(ex, sibling), device_id_type=MESH)

    moments = [
        pltpu.make_async_copy(one_ref, one, local_sem.at[0]),
        pltpu.make_async_copy(two_ref, two, local_sem.at[1]),
        pltpu.make_async_copy(flip_ref, flip, local_sem.at[2]),
    ]
    for copy in moments:
        copy.start()

    pl.semaphore_wait(barrier, EX - 1 + RING)

    def columns(chunk):
        return pl.ds(pl.multiple_of(chunk * CHUNK, CHUNK), CHUNK)

    def send_chunk(chunk, carry):
        for step, (dz, dy) in enumerate(STEPS):
            target = owner(dz, dy)
            pltpu.make_async_remote_copy(
                src_ref=g_ref.at[target, columns(chunk)],
                dst_ref=recv.at[ex, columns(chunk)],
                send_sem=send_sem.at[step],
                recv_sem=recv_sem.at[chunk],
                device_id=(target, bf),
                device_id_type=MESH,
            ).start()
        pltpu.make_async_copy(
            g_ref.at[ex, columns(chunk)], recv.at[ex, columns(chunk)], recv_sem.at[chunk]
        ).start()
        return carry

    lax.fori_loop(0, chunks, send_chunk, 0)

    device = ex * BF + bf
    for b in range(BF):
        source = b % RING * 2 + b // RING
        rows = rows_ref[:, source * width : (source + 1) * width]
        place = slice(b * width, (b + 1) * width)
        lanes = rows & (DEPTH - 1)
        index = lax.broadcasted_iota(jnp.int32, (16, width), 0)
        fine = parity_sign((lanes & 15) & index).astype(jnp.float32).astype(jnp.bfloat16)
        coarse = parity_sign((lanes >> 4) & index).astype(jnp.float32).astype(jnp.bfloat16)
        for i in range(16):
            weight[i * 16 : (i + 1) * 16, place] = fine * coarse[i : i + 1, :]
        sign_low[:, place] = parity_sign(((rows >> 8) & (ROWS - 1)) & index).astype(jnp.float32)
        index = lax.broadcasted_iota(jnp.int32, (chunks, width), 0)
        own = parity_sign((rows >> 15) & device)
        sign_high[:, place] = (own * parity_sign((rows >> 12) & (chunks - 1) & index)).astype(jnp.float32)
    part[...] = jnp.zeros_like(part)

    for copy in moments:
        copy.wait()

    def do_chunk(chunk, carry):
        pltpu.make_async_copy(recv.at[:, columns(chunk)], recv.at[:, columns(chunk)], recv_sem.at[chunk]).wait()
        for j in range(ROWS):
            span = pl.ds(pl.multiple_of(chunk * CHUNK + j * DEPTH, DEPTH), DEPTH)
            grad = recv[:, span]
            moment_new = BETA_ONE * one[:, span] + (1.0 - BETA_ONE) * grad
            second_new = BETA_TWO * two[:, span] + (1.0 - BETA_TWO) * grad * grad
            feature = flip[:, span].astype(jnp.float32) * moment_new * lax.rsqrt(second_new)
            top = feature.astype(jnp.bfloat16)
            high[j * 16 : (j + 1) * 16, :] = top
            low[j * 16 : (j + 1) * 16, :] = (feature - top.astype(jnp.float32)).astype(jnp.bfloat16)

        def tile(t, inner):
            place = pl.ds(pl.multiple_of(t * TILE, TILE), TILE)
            w = weight[:, place]
            product = jnp.dot(high[...], w, preferred_element_type=jnp.float32)
            product = product + jnp.dot(low[...], w, preferred_element_type=jnp.float32)
            sign = sign_low[:, place]
            total = product[0:16] * sign[0:1]
            for j in range(1, ROWS):
                total = total + product[j * 16 : (j + 1) * 16] * sign[j : j + 1]
            part[:, place] = part[:, place] + total * sign_high[pl.ds(chunk, 1), place]
            return inner

        return lax.fori_loop(0, count // TILE, tile, carry, unroll=4)

    lax.fori_loop(0, chunks, do_chunk, 0)

    span = count // 2
    to_core = pltpu.make_async_remote_copy(
        src_ref=part.at[:, pl.ds(pl.multiple_of((1 - core) * span, span), span)],
        dst_ref=got_core,
        send_sem=core_sem.at[0],
        recv_sem=core_sem.at[1],
        device_id=(ex, sibling),
        device_id_type=MESH,
    )
    to_core.start()
    to_core.wait()
    half[...] = part[:, pl.ds(pl.multiple_of(core * span, span), span)] + got_core[...]

    to_x = []
    for dx in (1, 2, 3):
        other = (x + dx) % RING
        copy = pltpu.make_async_remote_copy(
            src_ref=half.at[:, pl.ds(pl.multiple_of(other * width, width), width)],
            dst_ref=got_x.at[dx - 1],
            send_sem=x_send.at[dx - 1],
            recv_sem=x_recv.at[dx - 1],
            device_id=(ex, x_peer(dx)),
            device_id_type=MESH,
        )
        copy.start()
        to_x.append(copy)
    for copy in to_x:
        copy.wait()
    summed = half[:, pl.ds(pl.multiple_of(x * width, width), width)] + got_x[0] + got_x[1] + got_x[2]

    row = lax.broadcasted_iota(jnp.int32, (EX, width), 0)
    pooled = jnp.zeros((EX, width), jnp.float32)
    for e in range(EX):
        pooled = pooled + jnp.where(row == pool_ref[e], summed[e : e + 1], 0.0)
    mine[...] = pooled
    to_ex = []
    for step, (dz, dy) in enumerate(STEPS):
        target = owner(dz, dy)
        copy = pltpu.make_async_remote_copy(
            src_ref=mine.at[target],
            dst_ref=got_ex.at[ex],
            send_sem=ex_send,
            recv_sem=ex_recv,
            device_id=(target, bf),
            device_id_type=MESH,
        )
        copy.start()
    pltpu.make_async_copy(mine.at[ex], got_ex.at[ex], ex_recv).start()
    pltpu.make_async_copy(got_ex, got_ex, ex_recv).wait()
    scale = float(block_len * EX * BF) ** -0.5
    out_ref[...] = jnp.sum(got_ex[...], axis=0, keepdims=True) * scale
    for step in range(len(STEPS)):
        pltpu.make_async_copy(mine.at[0], mine.at[0], ex_send).wait()
        pltpu.make_async_copy(g_ref.at[0], g_ref.at[0], send_sem.at[step]).wait()


def per_device(gradients, moment_one, moment_two, rademacher, sample_rows, pool_order):
    block_len = moment_one.shape[0]
    count = sample_rows.shape[0]
    chunks = block_len // CHUNK
    width = count // BF
    dma = pltpu.SemaphoreType.DMA
    return pl.pallas_call(
        kernel,
        out_shape=jax.ShapeDtypeStruct((1, width), jnp.float32),
        in_specs=[pl.BlockSpec(memory_space=pl.ANY)] * 4
        + [pl.BlockSpec(memory_space=pltpu.VMEM), pl.BlockSpec(memory_space=pltpu.SMEM)],
        out_specs=pl.BlockSpec(memory_space=pltpu.VMEM),
        scratch_shapes=[
            pltpu.VMEM((EX, block_len), jnp.float32),
            pltpu.VMEM((1, block_len), jnp.float32),
            pltpu.VMEM((1, block_len), jnp.float32),
            pltpu.VMEM((1, block_len), jnp.int32),
            pltpu.VMEM((DEPTH, count), jnp.bfloat16),
            pltpu.VMEM((ROWS, count), jnp.float32),
            pltpu.VMEM((chunks, count), jnp.float32),
            pltpu.VMEM((ROWS * EX, DEPTH), jnp.bfloat16),
            pltpu.VMEM((ROWS * EX, DEPTH), jnp.bfloat16),
            pltpu.VMEM((EX, count), jnp.float32),
            pltpu.VMEM((EX, count // 2), jnp.float32),
            pltpu.VMEM((EX, count // 2), jnp.float32),
            pltpu.VMEM((RING - 1, EX, width), jnp.float32),
            pltpu.VMEM((EX, width), jnp.float32),
            pltpu.VMEM((EX, width), jnp.float32),
            dma((3,)),
            dma((len(STEPS),)),
            dma((chunks,)),
            dma((2,)),
            dma((RING - 1,)),
            dma((RING - 1,)),
            dma,
            dma,
        ],
        compiler_params=pltpu.CompilerParams(
            collective_id=0, has_side_effects=True, vmem_limit_bytes=56 * 2**20
        ),
    )(
        gradients.reshape(EX, block_len),
        moment_one.reshape(1, block_len),
        moment_two.reshape(1, block_len),
        rademacher.reshape(1, block_len),
        sample_rows.reshape(1, count),
        pool_order,
    )


def solution(mesh):
    in_specs = (P("ex", None, "bf"), P(("ex", "bf")), P(("ex", "bf")), P(("ex", "bf")), P(), P())
    out_specs = P("ex", "bf")
    return jax.shard_map(
        per_device, mesh=mesh, in_specs=in_specs, out_specs=out_specs, check_vma=False
    )
```

```python
import functools

import jax
import jax.numpy as jnp
from jax import lax
from jax.experimental import pallas as pl
from jax.experimental.pallas import tpu as pltpu
from jax.sharding import PartitionSpec as P

MESH = pl.DeviceIdType.MESH
BETA_ONE = 0.9
BETA_TWO = 0.999
RING = 4
EX = RING * RING
BF = 2 * RING
DEPTH = 256
ROWS = 16
CHUNK = DEPTH * ROWS

STEPS = [(2, 2), (1, 1), (3, 3), (2, 0), (0, 2), (1, 3), (3, 1), (2, 1), (1, 2), (2, 3), (3, 2), (0, 1), (1, 0), (0, 3), (3, 0)]


def parity_sign(values):
    values = values ^ (values >> 4)
    values = values ^ (values >> 2)
    values = values ^ (values >> 1)
    return 1 - 2 * (values & 1)


def kernel(
    g_ref, one_ref, two_ref, flip_ref, rows_ref, pool_ref, out_ref,
    recv, one, two, flip, weight, sign_low, sign_high, sign_row, high, low, part, outbox, inbox, mine, got_ex,
    g_send, g_recv, m_send, m_recv, bf_send, bf_recv, ex_send, ex_recv,
):
    ex = lax.axis_index("ex")
    bf = lax.axis_index("bf")
    z, y = ex // RING, ex % RING
    block_len = g_ref.shape[1]
    count = rows_ref.shape[1]
    side_len = block_len // 2
    chunks = side_len // CHUNK
    width = count // BF

    def owner(dz, dy):
        return (z + dz) % RING * RING + (y + dy) % RING

    barrier = pltpu.get_barrier_semaphore()
    for dz, dy in STEPS:
        pl.semaphore_signal(barrier, inc=1, device_id=(owner(dz, dy), bf), device_id_type=MESH)
    for d in range(1, BF):
        pl.semaphore_signal(barrier, inc=1, device_id=(ex, (bf + d) % BF), device_id_type=MESH)
    pl.semaphore_wait(barrier, EX - 1 + BF - 1)

    moments = ((one_ref, one), (two_ref, two), (flip_ref, flip))

    def send_chunk(chunk, carry):
        for side in (0, 1):
            own, other = (y, z) if side == 0 else (z, y)
            source = pl.ds(pl.multiple_of(side * side_len + chunk * CHUNK, CHUNK), CHUNK)
            place = pl.ds(pl.multiple_of(chunk * CHUNK, CHUNK), CHUNK)
            step = side * chunks + chunk
            for d in (2, 1, 3):
                along = (own + d) % RING
                target = z * RING + along if side == 0 else along * RING + y
                for i in range(RING):
                    row = i * RING + along if side == 0 else along * RING + i
                    pltpu.make_async_remote_copy(
                        src_ref=g_ref.at[row, source],
                        dst_ref=recv.at[side, i * RING + own, place],
                        send_sem=g_send,
                        recv_sem=g_recv.at[step],
                        device_id=(target, bf),
                        device_id_type=MESH,
                    ).start()
            for d in (2, 1, 3):
                along = (other + d) % RING
                target = along * RING + y if side == 0 else z * RING + along
                for k, (src, dst) in enumerate(moments):
                    pltpu.make_async_remote_copy(
                        src_ref=src.at[0, source],
                        dst_ref=dst.at[side, other, place],
                        send_sem=m_send.at[k],
                        recv_sem=m_recv.at[k, step],
                        device_id=(target, bf),
                        device_id_type=MESH,
                    ).start()
            for i in range(RING):
                row = i * RING + own if side == 0 else own * RING + i
                pltpu.make_async_copy(
                    g_ref.at[row, source], recv.at[side, i * RING + own, place], g_recv.at[step]
                ).start()
            for k, (src, dst) in enumerate(moments):
                pltpu.make_async_copy(src.at[0, source], dst.at[side, other, place], m_recv.at[k, step]).start()
        return carry

    lax.fori_loop(0, chunks, send_chunk, 0)

    for b in range(BF):
        place = slice(b * width, (b + 1) * width)
        rows = rows_ref[:, place]
        lanes = rows & (DEPTH - 1)
        block = rows >> 15
        index = lax.broadcasted_iota(jnp.int32, (16, width), 0)
        fine = parity_sign((lanes & 15) & index).astype(jnp.float32).astype(jnp.bfloat16)
        coarse = parity_sign((lanes >> 4) & index).astype(jnp.float32).astype(jnp.bfloat16)
        for i in range(16):
            weight[i * 16 : (i + 1) * 16, place] = fine * coarse[i : i + 1, :]
        sign_low[:, place] = parity_sign(((rows >> 8) & (ROWS - 1)) & index).astype(jnp.float32)
        index = lax.broadcasted_iota(jnp.int32, (chunks, width), 0)
        index_row = lax.broadcasted_iota(jnp.int32, (RING, width), 0)
        for side in (0, 1):
            own = parity_sign(block & (y * BF + bf if side == 0 else z * RING * BF + bf))
            step_sign = parity_sign((rows >> 12) & (side * chunks + index))
            sign_high[side, :, place] = (own * step_sign).astype(jnp.float32)
            other = (block >> 5 if side == 0 else block >> 3) & (RING - 1)
            sign_row[side, :, place] = parity_sign(other & index_row).astype(jnp.float32)
    part[...] = jnp.zeros_like(part)

    first = lax.broadcasted_iota(jnp.int32, (8, DEPTH), 0) < RING

    def features(side, chunk):
        step = side * chunks + chunk
        place = pl.ds(pl.multiple_of(chunk * CHUNK, CHUNK), CHUNK)
        whole = recv.at[side, :, place]
        pltpu.make_async_copy(whole, whole, g_recv.at[step]).wait()
        for k, (_, dst) in enumerate(moments):
            whole = dst.at[side, :, place]
            pltpu.make_async_copy(whole, whole, m_recv.at[k, step]).wait()
        for j in range(ROWS):
            span = pl.ds(pl.multiple_of(chunk * CHUNK + j * DEPTH, DEPTH), DEPTH)
            found = []
            for h in (0, 1):
                grad = recv[side, 8 * h : 8 * h + 8, span]

                def both(ref):
                    return jnp.where(first, ref[side, 2 * h : 2 * h + 1, span], ref[side, 2 * h + 1 : 2 * h + 2, span])

                moment_new = BETA_ONE * both(one) + (1.0 - BETA_ONE) * grad
                second_new = BETA_TWO * both(two) + (1.0 - BETA_TWO) * grad * grad
                found.append(both(flip).astype(jnp.float32) * moment_new * lax.rsqrt(second_new))
            feature = jnp.concatenate(found, axis=0)
            top = feature.astype(jnp.bfloat16)
            high[j * 16 : (j + 1) * 16, :] = top
            low[j * 16 : (j + 1) * 16, :] = (feature - top.astype(jnp.float32)).astype(jnp.bfloat16)

    def tile(side, chunk, t):
        place = pl.ds(pl.multiple_of(t * width, width), width)
        w = weight[:, place]
        product = jnp.dot(high[...], w, preferred_element_type=jnp.float32)
        product = product + jnp.dot(low[...], w, preferred_element_type=jnp.float32)
        sign = sign_low[:, place]
        total = product[0:16] * sign[0:1]
        for j in range(1, ROWS):
            total = total + product[j * 16 : (j + 1) * 16] * sign[j : j + 1]
        return part[side, :, place] + total * sign_high[side, pl.ds(chunk, 1), place]

    def step_chunk(step, carry):
        side, chunk = step % 2, step // 2
        features(side, chunk)
        for t in range(BF):
            part[side, :, t * width : (t + 1) * width] = tile(side, chunk, t)
        return carry

    lax.fori_loop(0, 2 * chunks - 1, step_chunk, 0)

    def by_example(side, total, place):
        sign = sign_row[side, :, place]
        found = total[0:RING] * sign[0:1]
        for i in range(1, RING):
            found = found + total[i * RING : (i + 1) * RING] * sign[i : i + 1]
        return found

    features(1, chunks - 1)
    sends = []
    for d in range(1, BF + 1):
        t = (bf + d) % BF
        place = pl.ds(pl.multiple_of(t * width, width), width)
        found = jnp.concatenate(
            [by_example(0, part[0, :, place], place), by_example(1, tile(1, chunks - 1, t), place)], axis=0
        )
        if d == BF:
            inbox[BF - 1] = found
        else:
            outbox[d - 1] = found
            copy = pltpu.make_async_remote_copy(
                src_ref=outbox.at[d - 1],
                dst_ref=inbox.at[d - 1],
                send_sem=bf_send.at[d - 1],
                recv_sem=bf_recv.at[d - 1],
                device_id=(ex, t),
                device_id_type=MESH,
            )
            copy.start()
            sends.append(copy)
    summed = inbox[BF - 1]
    for d, copy in enumerate(sends):
        copy.wait_recv()
        summed = summed + inbox[d]

    row = lax.broadcasted_iota(jnp.int32, (EX, width), 0)
    pooled = jnp.zeros((EX, width), jnp.float32)
    for i in range(RING):
        pooled = pooled + jnp.where(row == pool_ref[z * RING + i], summed[i : i + 1], 0.0)
        pooled = pooled + jnp.where(row == pool_ref[i * RING + y], summed[RING + i : RING + i + 1], 0.0)
    mine[...] = pooled
    for dz, dy in STEPS:
        target = owner(dz, dy)
        pltpu.make_async_remote_copy(
            src_ref=mine.at[target],
            dst_ref=got_ex.at[ex],
            send_sem=ex_send,
            recv_sem=ex_recv,
            device_id=(target, bf),
            device_id_type=MESH,
        ).start()
    pltpu.make_async_copy(mine.at[ex], got_ex.at[ex], ex_recv).start()
    for copy in sends:
        copy.wait_send()
    for part_rows in (8, 4):
        sent = g_ref.at[pl.ds(0, part_rows)]
        pltpu.make_async_copy(sent, sent, g_send).wait()
    for k, (src, _) in enumerate(moments):
        for _ in range(3):
            pltpu.make_async_copy(src, src, m_send.at[k]).wait()
    pltpu.make_async_copy(got_ex, got_ex, ex_recv).wait()
    scale = float(block_len * EX * BF) ** -0.5
    out_ref[...] = jnp.sum(got_ex[...], axis=0, keepdims=True) * scale
    for _ in STEPS:
        pltpu.make_async_copy(mine.at[0], mine.at[0], ex_send).wait()


def per_device(gradients, moment_one, moment_two, rademacher, sample_rows, pool_order):
    block_len = moment_one.shape[0]
    count = sample_rows.shape[0]
    side_len = block_len // 2
    chunks = side_len // CHUNK
    width = count // BF
    dma = pltpu.SemaphoreType.DMA
    return pl.pallas_call(
        kernel,
        out_shape=jax.ShapeDtypeStruct((1, width), jnp.float32),
        in_specs=[pl.BlockSpec(memory_space=pl.ANY)] * 4
        + [pl.BlockSpec(memory_space=pltpu.VMEM), pl.BlockSpec(memory_space=pltpu.SMEM)],
        out_specs=pl.BlockSpec(memory_space=pltpu.VMEM),
        scratch_shapes=[
            pltpu.VMEM((2, EX, side_len), jnp.float32),
            pltpu.VMEM((2, RING, side_len), jnp.float32),
            pltpu.VMEM((2, RING, side_len), jnp.float32),
            pltpu.VMEM((2, RING, side_len), jnp.int32),
            pltpu.VMEM((DEPTH, count), jnp.bfloat16),
            pltpu.VMEM((ROWS, count), jnp.float32),
            pltpu.VMEM((2, chunks, count), jnp.float32),
            pltpu.VMEM((2, RING, count), jnp.float32),
            pltpu.VMEM((ROWS * EX, DEPTH), jnp.bfloat16),
            pltpu.VMEM((ROWS * EX, DEPTH), jnp.bfloat16),
            pltpu.VMEM((2, EX, count), jnp.float32),
            pltpu.VMEM((BF - 1, 2 * RING, width), jnp.float32),
            pltpu.VMEM((BF, 2 * RING, width), jnp.float32),
            pltpu.VMEM((EX, width), jnp.float32),
            pltpu.VMEM((EX, width), jnp.float32),
            dma,
            dma((2 * chunks,)),
            dma((3,)),
            dma((3, 2 * chunks)),
            dma((BF - 1,)),
            dma((BF - 1,)),
            dma,
            dma,
        ],
        compiler_params=pltpu.CompilerParams(
            collective_id=0, has_side_effects=True, vmem_limit_bytes=56 * 2**20
        ),
    )(
        gradients.reshape(EX, block_len),
        moment_one.reshape(1, block_len),
        moment_two.reshape(1, block_len),
        rademacher.reshape(1, block_len),
        sample_rows.reshape(1, count),
        pool_order,
    )


def solution(mesh):
    in_specs = (P("ex", None, "bf"), P(("ex", "bf")), P(("ex", "bf")), P(("ex", "bf")), P(), P())
    out_specs = P("ex", "bf")
    return jax.shard_map(
        per_device, mesh=mesh, in_specs=in_specs, out_specs=out_specs, check_vma=False
    )
```

```python
import functools

import jax
import jax.numpy as jnp
from jax import lax
from jax.experimental import pallas as pl
from jax.experimental.pallas import tpu as pltpu
from jax.sharding import PartitionSpec as P

MESH = pl.DeviceIdType.MESH
BETA_ONE = 0.9
BETA_TWO = 0.999
RING = 4
EX = RING * RING
BF = 2 * RING
DEPTH = 256
ROWS = 16
CHUNK = DEPTH * ROWS

STEPS = [(2, 2), (1, 1), (3, 3), (2, 0), (0, 2), (1, 3), (3, 1), (2, 1), (1, 2), (2, 3), (3, 2), (0, 1), (1, 0), (0, 3), (3, 0)]


def parity_sign(values, bits):
    while bits > 1:
        bits = bits // 2
        values = values ^ (values >> bits)
    return (1 - 2 * (values & 1)).astype(jnp.float32)


def kernel(
    g_ref, one_ref, two_ref, flip_ref, rows_ref, pool_ref, out_ref,
    recv, one, two, flip, weight, coarse, sign_low, sign_high, sign_row, high, low, part, outbox, inbox, mine, got_ex,
    g_send, g_recv, m_send, m_recv, bf_send, bf_recv, ex_send, ex_recv,
):
    ex = lax.axis_index("ex")
    bf = lax.axis_index("bf")
    z, y = ex // RING, ex % RING
    block_len = g_ref.shape[1]
    count = rows_ref.shape[1]
    side_len = block_len // 2
    chunks = side_len // CHUNK
    width = count // BF

    def owner(dz, dy):
        return (z + dz) % RING * RING + (y + dy) % RING

    barrier = pltpu.get_barrier_semaphore()
    for dz, dy in STEPS:
        pl.semaphore_signal(barrier, inc=1, device_id=(owner(dz, dy), bf), device_id_type=MESH)
    for d in range(1, BF):
        pl.semaphore_signal(barrier, inc=1, device_id=(ex, (bf + d) % BF), device_id_type=MESH)
    pl.semaphore_wait(barrier, EX - 1 + BF - 1)

    moments = ((one_ref, one), (two_ref, two), (flip_ref, flip))

    def send_chunk(chunk):
        for side in (0, 1):
            own, other = (y, z) if side == 0 else (z, y)
            source = pl.ds(pl.multiple_of(side * side_len + chunk * CHUNK, CHUNK), CHUNK)
            place = pl.ds(pl.multiple_of(chunk * CHUNK, CHUNK), CHUNK)
            step = side * chunks + chunk
            for d in (2, 1, 3):
                along = (own + d) % RING
                target = z * RING + along if side == 0 else along * RING + y
                for i in range(RING):
                    row = i * RING + along if side == 0 else along * RING + i
                    pltpu.make_async_remote_copy(
                        src_ref=g_ref.at[row, source],
                        dst_ref=recv.at[side, i * RING + own, place],
                        send_sem=g_send,
                        recv_sem=g_recv.at[step],
                        device_id=(target, bf),
                        device_id_type=MESH,
                    ).start()
            for d in (2, 1, 3):
                along = (other + d) % RING
                target = along * RING + y if side == 0 else z * RING + along
                for k, (src, dst) in enumerate(moments):
                    pltpu.make_async_remote_copy(
                        src_ref=src.at[0, source],
                        dst_ref=dst.at[side, other, place],
                        send_sem=m_send.at[k],
                        recv_sem=m_recv.at[k, step],
                        device_id=(target, bf),
                        device_id_type=MESH,
                    ).start()
            for i in range(RING):
                row = i * RING + own if side == 0 else own * RING + i
                pltpu.make_async_copy(
                    g_ref.at[row, source], recv.at[side, i * RING + own, place], g_recv.at[step]
                ).start()
            for k, (src, dst) in enumerate(moments):
                pltpu.make_async_copy(src.at[0, source], dst.at[side, other, place], m_recv.at[k, step]).start()

    send_chunk(0)
    send_chunk(1)

    index = lax.broadcasted_iota(jnp.int32, (16, width), 0)
    member = lax.broadcasted_iota(jnp.int32, (8, width), 0)
    upper = member >= RING
    step_mask = jnp.where(upper, (z * RING * BF + bf) * block_len, (y * BF + bf) * block_len) + member * CHUNK
    row_mask = jnp.where(upper, (member - RING) * BF, member * BF * RING) * block_len

    def signs(b, carry):
        place = pl.ds(pl.multiple_of(b * width, width), width)
        rows = jnp.broadcast_to(rows_ref[:, place], (16, width))
        fine = parity_sign(rows & index, 4)
        coarse[...] = parity_sign((rows >> 4) & index, 4)
        for i in range(16):
            weight[i * 16 : (i + 1) * 16, place] = (fine * coarse[i : i + 1, :]).astype(jnp.bfloat16)
        sign_low[:, place] = parity_sign((rows >> 8) & index, 4)
        sign_high[:, place] = parity_sign(rows[:8] & step_mask, 32)
        sign_row[:, place] = parity_sign((rows[:8] & row_mask) >> 18, 4)
        return carry

    lax.fori_loop(0, BF, signs, 0)
    part[...] = jnp.zeros_like(part)

    first = lax.broadcasted_iota(jnp.int32, (8, DEPTH), 0) < RING

    def features(side, chunk):
        step = side * chunks + chunk
        place = pl.ds(pl.multiple_of(chunk * CHUNK, CHUNK), CHUNK)
        whole = recv.at[side, :, place]
        pltpu.make_async_copy(whole, whole, g_recv.at[step]).wait()
        for k, (_, dst) in enumerate(moments):
            whole = dst.at[side, :, place]
            pltpu.make_async_copy(whole, whole, m_recv.at[k, step]).wait()
        for j in range(ROWS):
            span = pl.ds(pl.multiple_of(chunk * CHUNK + j * DEPTH, DEPTH), DEPTH)
            found = []
            for h in (0, 1):
                grad = recv[side, 8 * h : 8 * h + 8, span]

                def both(ref):
                    return jnp.where(first, ref[side, 2 * h : 2 * h + 1, span], ref[side, 2 * h + 1 : 2 * h + 2, span])

                moment_new = BETA_ONE * both(one) + (1.0 - BETA_ONE) * grad
                second_new = BETA_TWO * both(two) + (1.0 - BETA_TWO) * grad * grad
                found.append(both(flip).astype(jnp.float32) * moment_new * lax.rsqrt(second_new))
            feature = jnp.concatenate(found, axis=0)
            top = feature.astype(jnp.bfloat16)
            high[j * 16 : (j + 1) * 16, :] = top
            low[j * 16 : (j + 1) * 16, :] = (feature - top.astype(jnp.float32)).astype(jnp.bfloat16)

    def tile(side, chunk, t):
        place = pl.ds(pl.multiple_of(t * width, width), width)
        w = weight[:, place]
        product = jnp.dot(high[...], w, preferred_element_type=jnp.float32)
        product = product + jnp.dot(low[...], w, preferred_element_type=jnp.float32)
        sign = sign_low[:, place]
        total = product[0:16] * sign[0:1]
        for j in range(1, ROWS):
            total = total + product[j * 16 : (j + 1) * 16] * sign[j : j + 1]
        return part[side, :, place] + total * sign_high[pl.ds(side * chunks + chunk, 1), place]

    def step_chunk(step, carry):
        side, chunk = step % 2, step // 2
        features(side, chunk)
        for t in range(BF):
            part[side, :, t * width : (t + 1) * width] = tile(side, chunk, t)

        @pl.when((side == 0) & (chunk + 2 < chunks))
        def _():
            send_chunk(chunk + 2)

        return carry

    lax.fori_loop(0, 2 * chunks - 1, step_chunk, 0)

    def by_example(side, total, place):
        sign = sign_row[side * RING : (side + 1) * RING, place]
        found = total[0:RING] * sign[0:1]
        for i in range(1, RING):
            found = found + total[i * RING : (i + 1) * RING] * sign[i : i + 1]
        return found

    features(1, chunks - 1)
    sends = []
    for d in range(1, BF + 1):
        t = (bf + d) % BF
        place = pl.ds(pl.multiple_of(t * width, width), width)
        found = jnp.concatenate(
            [by_example(0, part[0, :, place], place), by_example(1, tile(1, chunks - 1, t), place)], axis=0
        )
        if d == BF:
            inbox[BF - 1] = found
        else:
            outbox[d - 1] = found
            copy = pltpu.make_async_remote_copy(
                src_ref=outbox.at[d - 1],
                dst_ref=inbox.at[d - 1],
                send_sem=bf_send.at[d - 1],
                recv_sem=bf_recv.at[d - 1],
                device_id=(ex, t),
                device_id_type=MESH,
            )
            copy.start()
            sends.append(copy)
    summed = inbox[BF - 1]
    for d, copy in enumerate(sends):
        copy.wait_recv()
        summed = summed + inbox[d]

    row = lax.broadcasted_iota(jnp.int32, (EX, width), 0)
    pooled = jnp.zeros((EX, width), jnp.float32)
    for i in range(RING):
        pooled = pooled + jnp.where(row == pool_ref[z * RING + i], summed[i : i + 1], 0.0)
        pooled = pooled + jnp.where(row == pool_ref[i * RING + y], summed[RING + i : RING + i + 1], 0.0)
    mine[...] = pooled
    for dz, dy in STEPS:
        target = owner(dz, dy)
        pltpu.make_async_remote_copy(
            src_ref=mine.at[target],
            dst_ref=got_ex.at[ex],
            send_sem=ex_send,
            recv_sem=ex_recv,
            device_id=(target, bf),
            device_id_type=MESH,
        ).start()
    pltpu.make_async_copy(mine.at[ex], got_ex.at[ex], ex_recv).start()
    for copy in sends:
        copy.wait_send()
    for part_rows in (8, 4):
        sent = g_ref.at[pl.ds(0, part_rows)]
        pltpu.make_async_copy(sent, sent, g_send).wait()
    for k, (src, _) in enumerate(moments):
        for _ in range(3):
            pltpu.make_async_copy(src, src, m_send.at[k]).wait()
    pltpu.make_async_copy(got_ex, got_ex, ex_recv).wait()
    scale = float(block_len * EX * BF) ** -0.5
    out_ref[...] = jnp.sum(got_ex[...], axis=0, keepdims=True) * scale
    for _ in STEPS:
        pltpu.make_async_copy(mine.at[0], mine.at[0], ex_send).wait()


def per_device(gradients, moment_one, moment_two, rademacher, sample_rows, pool_order):
    block_len = moment_one.shape[0]
    count = sample_rows.shape[0]
    side_len = block_len // 2
    chunks = side_len // CHUNK
    width = count // BF
    dma = pltpu.SemaphoreType.DMA
    return pl.pallas_call(
        kernel,
        out_shape=jax.ShapeDtypeStruct((1, width), jnp.float32),
        in_specs=[pl.BlockSpec(memory_space=pl.ANY)] * 4
        + [pl.BlockSpec(memory_space=pltpu.VMEM), pl.BlockSpec(memory_space=pltpu.SMEM)],
        out_specs=pl.BlockSpec(memory_space=pltpu.VMEM),
        scratch_shapes=[
            pltpu.VMEM((2, EX, side_len), jnp.float32),
            pltpu.VMEM((2, RING, side_len), jnp.float32),
            pltpu.VMEM((2, RING, side_len), jnp.float32),
            pltpu.VMEM((2, RING, side_len), jnp.int32),
            pltpu.VMEM((DEPTH, count), jnp.bfloat16),
            pltpu.VMEM((16, width), jnp.float32),
            pltpu.VMEM((ROWS, count), jnp.float32),
            pltpu.VMEM((2 * chunks, count), jnp.float32),
            pltpu.VMEM((2 * RING, count), jnp.float32),
            pltpu.VMEM((ROWS * EX, DEPTH), jnp.bfloat16),
            pltpu.VMEM((ROWS * EX, DEPTH), jnp.bfloat16),
            pltpu.VMEM((2, EX, count), jnp.float32),
            pltpu.VMEM((BF - 1, 2 * RING, width), jnp.float32),
            pltpu.VMEM((BF, 2 * RING, width), jnp.float32),
            pltpu.VMEM((EX, width), jnp.float32),
            pltpu.VMEM((EX, width), jnp.float32),
            dma,
            dma((2 * chunks,)),
            dma((3,)),
            dma((3, 2 * chunks)),
            dma((BF - 1,)),
            dma((BF - 1,)),
            dma,
            dma,
        ],
        compiler_params=pltpu.CompilerParams(
            collective_id=0, has_side_effects=True, vmem_limit_bytes=56 * 2**20
        ),
    )(
        gradients.reshape(EX, block_len),
        moment_one.reshape(1, block_len),
        moment_two.reshape(1, block_len),
        rademacher.reshape(1, block_len),
        sample_rows.reshape(1, count),
        pool_order,
    )


def solution(mesh):
    in_specs = (P("ex", None, "bf"), P(("ex", "bf")), P(("ex", "bf")), P(("ex", "bf")), P(), P())
    out_specs = P("ex", "bf")
    return jax.shard_map(
        per_device, mesh=mesh, in_specs=in_specs, out_specs=out_specs, check_vma=False
    )
```

```python
import functools

import jax
import jax.numpy as jnp
from jax import lax
from jax.experimental import pallas as pl
from jax.experimental.pallas import tpu as pltpu
from jax.sharding import PartitionSpec as P

MESH = pl.DeviceIdType.MESH
BETA_ONE = 0.9
BETA_TWO = 0.999
RING = 4
EX = RING * RING
BF = 2 * RING
DEPTH = 256
GROUP = 16
PLAN = [(8, 2), (16, 2), (8, 1), (4, 2)]

STEPS = [(2, 2), (2, 1), (2, 3), (1, 2), (3, 2), (1, 1), (1, 3), (3, 1), (3, 3), (2, 0), (0, 2), (0, 1), (1, 0), (0, 3), (3, 0)]
TILES = [(2, 0), (2, 1), (1, 0), (1, 1), (3, 0), (3, 1), (0, 1)]


def parity_sign(values, bits):
    while bits > 1:
        bits = bits // 2
        values = values ^ (values >> bits)
    return (1 - 2 * (values & 1)).astype(jnp.float32)


def chunk_list():
    start = 0
    for spans, many in PLAN:
        for _ in range(many):
            yield spans, start
            start += spans


def kernel(
    g_ref, one_ref, two_ref, flip_ref, rows_ref, pool_ref, out_ref,
    recv, one, two, flip, weight, coarse, sign_low, sign_high, sign_row, left, part, outbox, inbox, mine, got_ex,
    g_send, g_recv, m_send, m_recv, bf_send, bf_recv, ex_send, ex_recv,
):
    ex = lax.axis_index("ex")
    bf = lax.axis_index("bf")
    z, y = ex // RING, ex % RING
    block_len = g_ref.shape[1]
    count = rows_ref.shape[1]
    side_len = block_len // 2
    width = count // BF
    order = list(chunk_list())

    def owner(dz, dy):
        return (z + dz) % RING * RING + (y + dy) % RING

    def bf_peer(dx, flip_core):
        core = bf % 2
        return (bf // 2 + dx) % RING * 2 + (1 - core if flip_core else core)

    barrier = pltpu.get_barrier_semaphore()
    for d in (2, 1, 3):
        pl.semaphore_signal(barrier, inc=1, device_id=(owner(d, 0), bf), device_id_type=MESH)
        pl.semaphore_signal(barrier, inc=1, device_id=(owner(0, d), bf), device_id_type=MESH)
    for dx, flip_core in TILES:
        pl.semaphore_signal(barrier, inc=1, device_id=(ex, bf_peer(dx, flip_core)), device_id_type=MESH)
    pl.semaphore_wait(barrier, 2 * (RING - 1) + BF - 1)

    moments = ((one_ref, one), (two_ref, two), (flip_ref, flip))

    def send_chunk(number, spans, first):
        size = spans * DEPTH
        for side in (0, 1):
            own, other = (y, z) if side == 0 else (z, y)
            source = pl.ds(side * side_len + first * DEPTH, size)
            place = pl.ds(first * DEPTH, size)
            for d in (2, 1, 3):
                along = (own + d) % RING
                target = z * RING + along if side == 0 else along * RING + y
                for i in range(RING):
                    row = i * RING + along if side == 0 else along * RING + i
                    pltpu.make_async_remote_copy(
                        src_ref=g_ref.at[row, source],
                        dst_ref=recv.at[side, i * RING + own, place],
                        send_sem=g_send,
                        recv_sem=g_recv.at[side, number],
                        device_id=(target, bf),
                        device_id_type=MESH,
                    ).start()
            for d in (2, 1, 3):
                along = (other + d) % RING
                target = along * RING + y if side == 0 else z * RING + along
                for k, (src, dst) in enumerate(moments):
                    pltpu.make_async_remote_copy(
                        src_ref=src.at[0, source],
                        dst_ref=dst.at[side, other, place],
                        send_sem=m_send.at[k],
                        recv_sem=m_recv.at[k, side, number],
                        device_id=(target, bf),
                        device_id_type=MESH,
                    ).start()
            for i in range(RING):
                row = i * RING + own if side == 0 else own * RING + i
                pltpu.make_async_copy(
                    g_ref.at[row, source], recv.at[side, i * RING + own, place], g_recv.at[side, number]
                ).start()
            for k, (src, dst) in enumerate(moments):
                pltpu.make_async_copy(
                    src.at[0, source], dst.at[side, other, place], m_recv.at[k, side, number]
                ).start()

    for number, (spans, first) in enumerate(order):
        send_chunk(number, spans, first)

    index = lax.broadcasted_iota(jnp.int32, (16, width), 0)
    member = lax.broadcasted_iota(jnp.int32, (8, width), 0)
    upper = member >= RING
    step_mask = jnp.where(upper, (z * RING * BF + bf) * block_len, (y * BF + bf) * block_len) + member * (GROUP * DEPTH)
    row_mask = jnp.where(upper, (member - RING) * BF, member * BF * RING) * block_len

    def signs(b, carry):
        place = pl.ds(pl.multiple_of(b * width, width), width)
        rows = jnp.broadcast_to(rows_ref[:, place], (16, width))
        fine = parity_sign(rows & index, 4)
        coarse[...] = parity_sign((rows >> 4) & index, 4)
        for i in range(16):
            weight[i * 16 : (i + 1) * 16, place] = (fine * coarse[i : i + 1, :]).astype(jnp.bfloat16)
        sign_low[:, place] = parity_sign((rows >> 8) & index, 4)
        sign_high[:, place] = parity_sign(rows[:8] & step_mask, 32)
        sign_row[:, place] = parity_sign((rows[:8] & row_mask) >> 18, 4)
        return carry

    lax.fori_loop(0, BF, signs, 0)
    part[...] = jnp.zeros_like(part)

    above = lax.broadcasted_iota(jnp.int32, (8, DEPTH), 0) < RING

    def features(side, number, spans, first):
        size = spans * DEPTH
        place = pl.ds(pl.multiple_of(first * DEPTH, 4 * DEPTH), size)
        whole = recv.at[side, :, place]
        pltpu.make_async_copy(whole, whole, g_recv.at[side, number]).wait()
        for k, (_, dst) in enumerate(moments):
            whole = dst.at[side, :, place]
            pltpu.make_async_copy(whole, whole, m_recv.at[k, side, number]).wait()
        for j in range(spans):
            span = pl.ds(pl.multiple_of((first + j) * DEPTH, DEPTH), DEPTH)
            found = []
            for h in (0, 1):
                grad = recv[side, 8 * h : 8 * h + 8, span]

                def both(ref):
                    return jnp.where(above, ref[side, 2 * h : 2 * h + 1, span], ref[side, 2 * h + 1 : 2 * h + 2, span])

                moment_new = BETA_ONE * both(one) + (1.0 - BETA_ONE) * grad
                second_new = BETA_TWO * both(two) + (1.0 - BETA_TWO) * grad * grad
                found.append(both(flip).astype(jnp.float32) * moment_new * lax.rsqrt(second_new))
            feature = jnp.concatenate(found, axis=0)
            top = feature.astype(jnp.bfloat16)
            left[j * 16 : (j + 1) * 16, :] = top
            rest = (feature - top.astype(jnp.float32)).astype(jnp.bfloat16)
            left[(spans + j) * 16 : (spans + j + 1) * 16, :] = rest

    def tile(side, spans, first, t):
        place = pl.ds(pl.multiple_of(t * width, width), width)
        w = weight[:, place]
        product = jnp.dot(left[: 2 * spans * 16], w, preferred_element_type=jnp.float32)
        product = product[: spans * 16] + product[spans * 16 :]
        sign = sign_low[pl.ds(pl.multiple_of(first % GROUP // 8 * 8, 8), max(spans, 8)), place]
        if spans == 4:
            sign = jnp.where(first % 8 == 4, sign[4:8], sign[0:4])
        total = product[0:16] * sign[0:1]
        for j in range(1, spans):
            total = total + product[j * 16 : (j + 1) * 16] * sign[j : j + 1]
        step_sign = sign_high[pl.ds(side * (side_len // (GROUP * DEPTH)) + first // GROUP, 1), place]
        return part[side, :, place] + total * step_sign

    def do_chunk(side, number, spans, first):
        features(side, number, spans, first)
        for t in range(BF):
            part[side, :, t * width : (t + 1) * width] = tile(side, spans, first, t)

    def by_example(side, total, place):
        sign = sign_row[side * RING : (side + 1) * RING, place]
        found = total[0:RING] * sign[0:1]
        for i in range(1, RING):
            found = found + total[i * RING : (i + 1) * RING] * sign[i : i + 1]
        return found

    def bf_copy(side, slot):
        return pltpu.make_async_remote_copy(
            src_ref=outbox.at[side, slot],
            dst_ref=inbox.at[side, slot],
            send_sem=bf_send.at[side, slot],
            recv_sem=bf_recv.at[side, slot],
            device_id=(ex, bf_peer(*TILES[slot])),
            device_id_type=MESH,
        )

    number, start = 0, 0
    for spans, many in PLAN:

        def step_chunk(step, carry, spans=spans, number=number, start=start):
            do_chunk(step % 2, number + step // 2, spans, start + step // 2 * spans)
            return carry

        steps = 2 * many - (2 if number + many == len(order) else 0)
        lax.fori_loop(0, steps, step_chunk, 0)
        number, start = number + many, start + many * spans

    number, (spans, first) = len(order) - 1, order[-1]
    tiles = [bf_peer(*peer) for peer in TILES] + [bf]
    do_chunk(0, number, spans, first)
    for side in (0, 1):
        if side == 1:
            features(side, number, spans, first)
        for slot, t in enumerate(tiles):
            place = pl.ds(pl.multiple_of(t * width, width), width)
            total = part[side, :, place] if side == 0 else tile(side, spans, first, t)
            if slot < len(TILES):
                outbox[side, slot] = by_example(side, total, place)
                bf_copy(side, slot).start()
            else:
                inbox[side, slot] = by_example(side, total, place)
    summed = []
    for side in (0, 1):
        found = inbox[side, BF - 1]
        for slot in range(BF - 1):
            bf_copy(side, slot).wait_recv()
            found = found + inbox[side, slot]
        summed.append(found)

    row = lax.broadcasted_iota(jnp.int32, (EX, width), 0)
    pooled = jnp.zeros((EX, width), jnp.float32)
    for i in range(RING):
        pooled = pooled + jnp.where(row == pool_ref[z * RING + i], summed[0][i : i + 1], 0.0)
        pooled = pooled + jnp.where(row == pool_ref[i * RING + y], summed[1][i : i + 1], 0.0)
    mine[...] = pooled
    for dz, dy in STEPS:
        target = owner(dz, dy)
        pltpu.make_async_remote_copy(
            src_ref=mine.at[target],
            dst_ref=got_ex.at[ex],
            send_sem=ex_send,
            recv_sem=ex_recv,
            device_id=(target, bf),
            device_id_type=MESH,
        ).start()
    pltpu.make_async_copy(mine.at[ex], got_ex.at[ex], ex_recv).start()
    for side in (0, 1):
        for slot in range(BF - 1):
            bf_copy(side, slot).wait_send()
    for part_rows in (8, 4):
        sent = g_ref.at[pl.ds(0, part_rows)]
        pltpu.make_async_copy(sent, sent, g_send).wait()
    for k, (src, _) in enumerate(moments):
        for _ in range(3):
            pltpu.make_async_copy(src, src, m_send.at[k]).wait()
    pltpu.make_async_copy(got_ex, got_ex, ex_recv).wait()
    scale = float(block_len * EX * BF) ** -0.5
    out_ref[...] = jnp.sum(got_ex[...], axis=0, keepdims=True) * scale
    for _ in STEPS:
        pltpu.make_async_copy(mine.at[0], mine.at[0], ex_send).wait()


def per_device(gradients, moment_one, moment_two, rademacher, sample_rows, pool_order):
    block_len = moment_one.shape[0]
    count = sample_rows.shape[0]
    side_len = block_len // 2
    width = count // BF
    chunks = len(list(chunk_list()))
    dma = pltpu.SemaphoreType.DMA
    return pl.pallas_call(
        kernel,
        out_shape=jax.ShapeDtypeStruct((1, width), jnp.float32),
        in_specs=[pl.BlockSpec(memory_space=pl.ANY)] * 4
        + [pl.BlockSpec(memory_space=pltpu.VMEM), pl.BlockSpec(memory_space=pltpu.SMEM)],
        out_specs=pl.BlockSpec(memory_space=pltpu.VMEM),
        scratch_shapes=[
            pltpu.VMEM((2, EX, side_len), jnp.float32),
            pltpu.VMEM((2, RING, side_len), jnp.float32),
            pltpu.VMEM((2, RING, side_len), jnp.float32),
            pltpu.VMEM((2, RING, side_len), jnp.int32),
            pltpu.VMEM((DEPTH, count), jnp.bfloat16),
            pltpu.VMEM((16, width), jnp.float32),
            pltpu.VMEM((GROUP, count), jnp.float32),
            pltpu.VMEM((block_len // (GROUP * DEPTH), count), jnp.float32),
            pltpu.VMEM((2 * RING, count), jnp.float32),
            pltpu.VMEM((2 * GROUP * EX, DEPTH), jnp.bfloat16),
            pltpu.VMEM((2, EX, count), jnp.float32),
            pltpu.VMEM((2, BF - 1, RING, width), jnp.float32),
            pltpu.VMEM((2, BF, RING, width), jnp.float32),
            pltpu.VMEM((EX, width), jnp.float32),
            pltpu.VMEM((EX, width), jnp.float32),
            dma,
            dma((2, chunks)),
            dma((3,)),
            dma((3, 2, chunks)),
            dma((2, BF - 1)),
            dma((2, BF - 1)),
            dma,
            dma,
        ],
        compiler_params=pltpu.CompilerParams(
            collective_id=0, has_side_effects=True, vmem_limit_bytes=56 * 2**20
        ),
    )(
        gradients.reshape(EX, block_len),
        moment_one.reshape(1, block_len),
        moment_two.reshape(1, block_len),
        rademacher.reshape(1, block_len),
        sample_rows.reshape(1, count),
        pool_order,
    )


def solution(mesh):
    in_specs = (P("ex", None, "bf"), P(("ex", "bf")), P(("ex", "bf")), P(("ex", "bf")), P(), P())
    out_specs = P("ex", "bf")
    return jax.shard_map(
        per_device, mesh=mesh, in_specs=in_specs, out_specs=out_specs, check_vma=False
    )
```

```python
import functools

import jax
import jax.numpy as jnp
from jax import lax
from jax.experimental import pallas as pl
from jax.experimental.pallas import tpu as pltpu
from jax.sharding import PartitionSpec as P

MESH = pl.DeviceIdType.MESH
BETA_ONE = 0.9
BETA_TWO = 0.999
RING = 4
EX = RING * RING
BF = 2 * RING
DEPTH = 256
GROUP = 16
PLAN = [(8, 2), (16, 2), (8, 2)]
LANES = 128
TILE = 256

STEPS = [(2, 2), (2, 1), (2, 3), (1, 2), (3, 2), (1, 1), (1, 3), (3, 1), (3, 3), (2, 0), (0, 2), (0, 1), (1, 0), (0, 3), (3, 0)]
TILES = [(2, 0), (2, 1), (1, 0), (1, 1), (3, 0), (3, 1), (0, 1)]


def parity_sign(values, bits):
    while bits > 1:
        bits = bits // 2
        values = values ^ (values >> bits)
    return (1 - 2 * (values & 1)).astype(jnp.float32)


def chunk_list():
    start = 0
    for spans, many in PLAN:
        for _ in range(many):
            yield spans, start
            start += spans


def kernel(
    g_ref, one_ref, two_ref, flip_ref, rows_ref, pool_ref, out_ref,
    recv, one, two, flip, weight, coarse, sign_low, sign_high, sign_row, left, slots, unsort, which, part, outbox, inbox, mine, got_ex,
    g_send, g_recv, m_send, m_recv, bf_send, bf_recv, ex_send, ex_recv,
):
    ex = lax.axis_index("ex")
    bf = lax.axis_index("bf")
    z, y = ex // RING, ex % RING
    block_len = g_ref.shape[1]
    count = rows_ref.shape[1]
    side_len = block_len // 2
    width = count // BF
    slotted = width + TILE
    order = list(chunk_list())

    def owner(dz, dy):
        return (z + dz) % RING * RING + (y + dy) % RING

    def bf_peer(dx, flip_core):
        core = bf % 2
        return (bf // 2 + dx) % RING * 2 + (1 - core if flip_core else core)

    barrier = pltpu.get_barrier_semaphore()
    for d in (2, 1, 3):
        pl.semaphore_signal(barrier, inc=1, device_id=(owner(d, 0), bf), device_id_type=MESH)
        pl.semaphore_signal(barrier, inc=1, device_id=(owner(0, d), bf), device_id_type=MESH)
    for dx, flip_core in TILES:
        pl.semaphore_signal(barrier, inc=1, device_id=(ex, bf_peer(dx, flip_core)), device_id_type=MESH)
    pl.semaphore_wait(barrier, 2 * (RING - 1) + BF - 1)

    moments = ((one_ref, one), (two_ref, two), (flip_ref, flip))

    def send_chunk(number, spans, first):
        size = spans * DEPTH
        for side in (0, 1):
            own, other = (y, z) if side == 0 else (z, y)
            source = pl.ds(side * side_len + first * DEPTH, size)
            place = pl.ds(first * DEPTH, size)
            for d in (2, 1, 3):
                along = (own + d) % RING
                target = z * RING + along if side == 0 else along * RING + y
                for i in range(RING):
                    row = i * RING + along if side == 0 else along * RING + i
                    pltpu.make_async_remote_copy(
                        src_ref=g_ref.at[row, source],
                        dst_ref=recv.at[side, i * RING + own, place],
                        send_sem=g_send,
                        recv_sem=g_recv.at[side, number],
                        device_id=(target, bf),
                        device_id_type=MESH,
                    ).start()
            for d in (2, 1, 3):
                along = (other + d) % RING
                target = along * RING + y if side == 0 else z * RING + along
                for k, (src, dst) in enumerate(moments):
                    pltpu.make_async_remote_copy(
                        src_ref=src.at[0, source],
                        dst_ref=dst.at[side, other, place],
                        send_sem=m_send.at[k],
                        recv_sem=m_recv.at[k, side, number],
                        device_id=(target, bf),
                        device_id_type=MESH,
                    ).start()
            for i in range(RING):
                row = i * RING + own if side == 0 else own * RING + i
                pltpu.make_async_copy(
                    g_ref.at[row, source], recv.at[side, i * RING + own, place], g_recv.at[side, number]
                ).start()
            for k, (src, dst) in enumerate(moments):
                pltpu.make_async_copy(
                    src.at[0, source], dst.at[side, other, place], m_recv.at[k, side, number]
                ).start()

    for number, (spans, first) in enumerate(order):
        send_chunk(number, spans, first)

    codes = jnp.concatenate([rows_ref[:, b * width : (b + 1) * width] for b in range(BF)], axis=0)
    bit = (codes >> 8) & 1
    before = lax.broadcasted_iota(jnp.int32, (LANES, LANES), 0) < lax.broadcasted_iota(jnp.int32, (LANES, LANES), 1)
    before = jnp.where(before, 1.0, 0.0).astype(jnp.bfloat16)
    ones = jnp.zeros((BF, 1), jnp.float32)
    ranks = []
    for b in range(width // LANES):
        piece = bit[:, b * LANES : (b + 1) * LANES].astype(jnp.float32)
        ranks.append(jnp.dot(piece.astype(jnp.bfloat16), before, preferred_element_type=jnp.float32) + ones)
        ones = ones + jnp.sum(piece, axis=1, keepdims=True)
    rank = jnp.concatenate(ranks, axis=1).astype(jnp.int32)
    zeros = width - ones.astype(jnp.int32)
    lane = lax.broadcasted_iota(jnp.int32, (BF, width), 1)
    slots[...] = jnp.where(bit == 1, TILE + zeros + rank, lane - rank)
    for b in range(BF):
        zero_count = width - jnp.sum(bit[b : b + 1])
        for u in range(slotted // TILE):
            which[b * (slotted // TILE) + u] = (u * TILE >= zero_count).astype(jnp.int32)

    def one_hot(slot):
        index = lax.broadcasted_iota(jnp.int32, (LANES, width), 0)
        return jnp.where(index == (slot & (LANES - 1)), 1.0, 0.0).astype(jnp.bfloat16)

    index = lax.broadcasted_iota(jnp.int32, (16, slotted), 0)
    member = lax.broadcasted_iota(jnp.int32, (8, slotted), 0)
    upper = member >= RING
    step_mask = jnp.where(upper, (z * RING * BF + bf) * block_len, (y * BF + bf) * block_len) + member * (GROUP * DEPTH)
    row_mask = jnp.where(upper, (member - RING) * BF, member * BF * RING) * block_len

    def signs(b, carry):
        code = rows_ref[:, pl.ds(pl.multiple_of(b * width, width), width)]
        slot = slots[pl.ds(b, 1), :]
        here = lax.broadcasted_iota(jnp.int32, (16, width), 0) == (slot >> 7)
        pieces = [jnp.where(here, (code >> shift) & 255, 0).astype(jnp.float32) for shift in (0, 8, 16)]
        pieces = jnp.concatenate(pieces, axis=0).astype(jnp.bfloat16)
        moved = lax.dot_general(
            pieces, one_hot(slot), (((1,), (1,)), ((), ())), preferred_element_type=jnp.float32
        ).astype(jnp.int32)
        moved = moved[0:16] + (moved[16:32] << 8) + (moved[32:48] << 16)
        rows = jnp.concatenate([moved[i : i + 1] for i in range(slotted // LANES)], axis=1)
        rows = jnp.broadcast_to(rows, (16, slotted))
        place = pl.ds(pl.multiple_of(b * slotted, slotted), slotted)
        fine = parity_sign(rows & index, 4)
        coarse[...] = parity_sign((rows >> 4) & index, 4)
        for i in range(16):
            weight[i * 16 : (i + 1) * 16, place] = (fine * coarse[i : i + 1, :]).astype(jnp.bfloat16)
        sign_low[:, place] = parity_sign((rows[:8] >> 9) & (index[:8] & 7), 4)
        sign_high[:, place] = parity_sign(rows[:8] & step_mask, 32)
        sign_row[:, place] = parity_sign((rows[:8] & row_mask) >> 18, 4)
        return carry

    lax.fori_loop(0, BF, signs, 0, unroll=2)
    unsort[...] = one_hot(slots[pl.ds(bf, 1), :])
    part[...] = jnp.zeros_like(part)

    above = lax.broadcasted_iota(jnp.int32, (8, DEPTH), 0) < RING

    def features(side, number, spans, first):
        size = spans * DEPTH
        place = pl.ds(pl.multiple_of(first * DEPTH, 4 * DEPTH), size)
        whole = recv.at[side, :, place]
        pltpu.make_async_copy(whole, whole, g_recv.at[side, number]).wait()
        for k, (_, dst) in enumerate(moments):
            whole = dst.at[side, :, place]
            pltpu.make_async_copy(whole, whole, m_recv.at[k, side, number]).wait()
        def feature(j):
            span = pl.ds(pl.multiple_of((first + j) * DEPTH, DEPTH), DEPTH)
            found = []
            for h in (0, 1):
                grad = recv[side, 8 * h : 8 * h + 8, span]

                def both(ref):
                    return jnp.where(above, ref[side, 2 * h : 2 * h + 1, span], ref[side, 2 * h + 1 : 2 * h + 2, span])

                moment_new = BETA_ONE * both(one) + (1.0 - BETA_ONE) * grad
                second_new = BETA_TWO * both(two) + (1.0 - BETA_TWO) * grad * grad
                found.append(both(flip).astype(jnp.float32) * moment_new * lax.rsqrt(second_new))
            return jnp.concatenate(found, axis=0)

        for q in range(spans // 2):
            even, odd = feature(2 * q), feature(2 * q + 1)
            for value, combined in ((0, even + odd), (1, even - odd)):
                top = combined.astype(jnp.bfloat16)
                rest = (combined - top.astype(jnp.float32)).astype(jnp.bfloat16)
                left[value, q * 16 : (q + 1) * 16, :] = top
                at = (spans // 2 + q) * 16
                left[value, at : at + 16, :] = rest

    def tile(side, spans, first, t):
        half = spans // 2
        found = []
        for u in range(slotted // TILE):
            place = pl.ds(pl.multiple_of(t * slotted + u * TILE, TILE), TILE)
            value = which[t * (slotted // TILE) + u]
            rows = left[value, : spans * 16, :]
            product = jnp.dot(rows, weight[:, place], preferred_element_type=jnp.float32)
            product = product[: half * 16] + product[half * 16 :]
            sign = sign_low[:, place]
            if spans < GROUP:
                sign = jnp.where(first % GROUP == 8, sign[4:8], sign[0:4])
            total = product[0:16] * sign[0:1]
            for j in range(1, half):
                total = total + product[j * 16 : (j + 1) * 16] * sign[j : j + 1]
            step_sign = sign_high[pl.ds(side * (side_len // (GROUP * DEPTH)) + first // GROUP, 1), place]
            found.append(part[side, :, place] + total * step_sign)
        return jnp.concatenate(found, axis=1)

    def do_chunk(side, number, spans, first):
        features(side, number, spans, first)
        for t in range(BF):
            part[side, :, t * slotted : (t + 1) * slotted] = tile(side, spans, first, t)

    def by_example(side, total, place):
        sign = sign_row[side * RING : (side + 1) * RING, place]
        found = total[0:RING] * sign[0:1]
        for i in range(1, RING):
            found = found + total[i * RING : (i + 1) * RING] * sign[i : i + 1]
        return found

    def bf_copy(side, slot):
        return pltpu.make_async_remote_copy(
            src_ref=outbox.at[side, slot],
            dst_ref=inbox.at[side, slot],
            send_sem=bf_send.at[side, slot],
            recv_sem=bf_recv.at[side, slot],
            device_id=(ex, bf_peer(*TILES[slot])),
            device_id_type=MESH,
        )

    number, start = 0, 0
    for spans, many in PLAN:

        def step_chunk(step, carry, spans=spans, number=number, start=start):
            do_chunk(step % 2, number + step // 2, spans, start + step // 2 * spans)
            return carry

        steps = 2 * many - (2 if number + many == len(order) else 0)
        lax.fori_loop(0, steps, step_chunk, 0)
        number, start = number + many, start + many * spans

    number, (spans, first) = len(order) - 1, order[-1]
    tiles = [bf_peer(*peer) for peer in TILES] + [bf]
    do_chunk(0, number, spans, first)
    for side in (0, 1):
        if side == 1:
            features(side, number, spans, first)
        for slot, t in enumerate(tiles):
            place = pl.ds(pl.multiple_of(t * slotted, slotted), slotted)
            total = part[side, :, place] if side == 0 else tile(side, spans, first, t)
            if slot < len(TILES):
                outbox[side, slot] = by_example(side, total, place)
                bf_copy(side, slot).start()
            else:
                inbox[side, slot] = by_example(side, total, place)
    summed = []
    for side in (0, 1):
        found = inbox[side, BF - 1]
        for slot in range(BF - 1):
            bf_copy(side, slot).wait_recv()
            found = found + inbox[side, slot]
        summed.append(found)

    found = jnp.concatenate(summed, axis=0)
    terms = []
    for _ in range(3):
        term = found.astype(jnp.bfloat16).astype(jnp.float32)
        found = found - term
        terms += [term[:, i * LANES : (i + 1) * LANES] for i in range(slotted // LANES)]
    stacked = jnp.concatenate(terms, axis=0).astype(jnp.bfloat16)
    spread = jnp.dot(stacked, unsort[...], preferred_element_type=jnp.float32)
    size = slotted // LANES * 8
    spread = spread[:size] + spread[size : 2 * size] + spread[2 * size :]
    chosen = jnp.broadcast_to(slots[pl.ds(bf, 1), :] >> 7, (8, width))
    summed = jnp.zeros((8, width), jnp.float32)
    for i in range(slotted // LANES):
        summed = summed + jnp.where(chosen == i, spread[8 * i : 8 * i + 8], 0.0)

    row = lax.broadcasted_iota(jnp.int32, (EX, width), 0)
    pooled = jnp.zeros((EX, width), jnp.float32)
    for i in range(RING):
        pooled = pooled + jnp.where(row == pool_ref[z * RING + i], summed[i : i + 1], 0.0)
        pooled = pooled + jnp.where(row == pool_ref[i * RING + y], summed[RING + i : RING + i + 1], 0.0)
    mine[...] = pooled
    for dz, dy in STEPS:
        target = owner(dz, dy)
        pltpu.make_async_remote_copy(
            src_ref=mine.at[target],
            dst_ref=got_ex.at[ex],
            send_sem=ex_send,
            recv_sem=ex_recv,
            device_id=(target, bf),
            device_id_type=MESH,
        ).start()
    pltpu.make_async_copy(mine.at[ex], got_ex.at[ex], ex_recv).start()
    for side in (0, 1):
        for slot in range(BF - 1):
            bf_copy(side, slot).wait_send()
    for part_rows in (8, 4):
        sent = g_ref.at[pl.ds(0, part_rows)]
        pltpu.make_async_copy(sent, sent, g_send).wait()
    for k, (src, _) in enumerate(moments):
        for _ in range(3):
            pltpu.make_async_copy(src, src, m_send.at[k]).wait()
    pltpu.make_async_copy(got_ex, got_ex, ex_recv).wait()
    scale = float(block_len * EX * BF) ** -0.5
    out_ref[...] = jnp.sum(got_ex[...], axis=0, keepdims=True) * scale
    for _ in STEPS:
        pltpu.make_async_copy(mine.at[0], mine.at[0], ex_send).wait()


def per_device(gradients, moment_one, moment_two, rademacher, sample_rows, pool_order):
    block_len = moment_one.shape[0]
    count = sample_rows.shape[0]
    side_len = block_len // 2
    width = count // BF
    slotted = width + TILE
    slot_count = slotted * BF
    chunks = len(list(chunk_list()))
    dma = pltpu.SemaphoreType.DMA
    return pl.pallas_call(
        kernel,
        out_shape=jax.ShapeDtypeStruct((1, width), jnp.float32),
        in_specs=[pl.BlockSpec(memory_space=pl.ANY)] * 4
        + [pl.BlockSpec(memory_space=pltpu.VMEM), pl.BlockSpec(memory_space=pltpu.SMEM)],
        out_specs=pl.BlockSpec(memory_space=pltpu.VMEM),
        scratch_shapes=[
            pltpu.VMEM((2, EX, side_len), jnp.float32),
            pltpu.VMEM((2, RING, side_len), jnp.float32),
            pltpu.VMEM((2, RING, side_len), jnp.float32),
            pltpu.VMEM((2, RING, side_len), jnp.int32),
            pltpu.VMEM((DEPTH, slot_count), jnp.bfloat16),
            pltpu.VMEM((16, slotted), jnp.float32),
            pltpu.VMEM((GROUP // 2, slot_count), jnp.float32),
            pltpu.VMEM((block_len // (GROUP * DEPTH), slot_count), jnp.float32),
            pltpu.VMEM((2 * RING, slot_count), jnp.float32),
            pltpu.VMEM((2, GROUP * EX, DEPTH), jnp.bfloat16),
            pltpu.VMEM((BF, width), jnp.int32),
            pltpu.VMEM((LANES, width), jnp.bfloat16),
            pltpu.SMEM((slot_count // TILE,), jnp.int32),
            pltpu.VMEM((2, EX, slot_count), jnp.float32),
            pltpu.VMEM((2, BF - 1, RING, slotted), jnp.float32),
            pltpu.VMEM((2, BF, RING, slotted), jnp.float32),
            pltpu.VMEM((EX, width), jnp.float32),
            pltpu.VMEM((EX, width), jnp.float32),
            dma,
            dma((2, chunks)),
            dma((3,)),
            dma((3, 2, chunks)),
            dma((2, BF - 1)),
            dma((2, BF - 1)),
            dma,
            dma,
        ],
        compiler_params=pltpu.CompilerParams(
            collective_id=0, has_side_effects=True, vmem_limit_bytes=56 * 2**20
        ),
    )(
        gradients.reshape(EX, block_len),
        moment_one.reshape(1, block_len),
        moment_two.reshape(1, block_len),
        rademacher.reshape(1, block_len),
        sample_rows.reshape(1, count),
        pool_order,
    )


def solution(mesh):
    in_specs = (P("ex", None, "bf"), P(("ex", "bf")), P(("ex", "bf")), P(("ex", "bf")), P(), P())
    out_specs = P("ex", "bf")
    return jax.shard_map(
        per_device, mesh=mesh, in_specs=in_specs, out_specs=out_specs, check_vma=False
    )
```

```python
import functools

import jax
import jax.numpy as jnp
from jax import lax
from jax.experimental import pallas as pl
from jax.experimental.pallas import tpu as pltpu
from jax.sharding import PartitionSpec as P

MESH = pl.DeviceIdType.MESH
BETA_ONE = 0.9
BETA_TWO = 0.999
RING = 4
EX = RING * RING
BF = 2 * RING
DEPTH = 256
GROUP = 16
PLAN = [(8, 2), (16, 2), (8, 2)]
LANES = 128
TILE = 256

STEPS = [(2, 2), (2, 1), (2, 3), (1, 2), (3, 2), (1, 1), (1, 3), (3, 1), (3, 3), (2, 0), (0, 2), (0, 1), (1, 0), (0, 3), (3, 0)]
TILES = [(2, 0), (2, 1), (1, 0), (1, 1), (3, 0), (3, 1), (0, 1)]


def parity_sign(values, bits):
    while bits > 1:
        bits = bits // 2
        values = values ^ (values >> bits)
    return (1 - 2 * (values & 1)).astype(jnp.float32)


def chunk_list():
    start = 0
    for spans, many in PLAN:
        for _ in range(many):
            yield spans, start
            start += spans


def kernel(
    g_ref, one_ref, two_ref, flip_ref, rows_hbm, pool_hbm, out_ref,
    rows_ref, pool_ref, recv, one, two, flip, weight, coarse, sign_low, sign_high, sign_row, left, slots, unsort, which, part, outbox, inbox, mine, got_ex,
    g_send, g_recv, m_send, m_recv, bf_send, bf_recv, ex_send, ex_recv, local_sem,
):
    ex = lax.axis_index("ex")
    bf = lax.axis_index("bf")
    z, y = ex // RING, ex % RING
    block_len = g_ref.shape[1]
    count = rows_hbm.shape[1]
    side_len = block_len // 2
    width = count // BF
    slotted = width + TILE
    order = list(chunk_list())

    def owner(dz, dy):
        return (z + dz) % RING * RING + (y + dy) % RING

    def bf_peer(dx, flip_core):
        core = bf % 2
        return (bf // 2 + dx) % RING * 2 + (1 - core if flip_core else core)

    samples = pltpu.make_async_copy(rows_hbm, rows_ref, local_sem.at[0])
    pools = pltpu.make_async_copy(pool_hbm, pool_ref, local_sem.at[1])

    barrier = pltpu.get_barrier_semaphore()
    for d in (2, 1, 3):
        pl.semaphore_signal(barrier, inc=1, device_id=(owner(d, 0), bf), device_id_type=MESH)
        pl.semaphore_signal(barrier, inc=1, device_id=(owner(0, d), bf), device_id_type=MESH)
    for dx, flip_core in TILES:
        pl.semaphore_signal(barrier, inc=1, device_id=(ex, bf_peer(dx, flip_core)), device_id_type=MESH)
    samples.start()
    pools.start()
    pl.semaphore_wait(barrier, 2 * (RING - 1) + BF - 1)

    moments = ((one_ref, one), (two_ref, two), (flip_ref, flip))

    def send_chunk(number, spans, first):
        size = spans * DEPTH
        for side in (0, 1):
            own, other = (y, z) if side == 0 else (z, y)
            source = pl.ds(side * side_len + first * DEPTH, size)
            place = pl.ds(first * DEPTH, size)
            for d in (2, 1, 3):
                along = (own + d) % RING
                target = z * RING + along if side == 0 else along * RING + y
                for i in range(RING):
                    row = i * RING + along if side == 0 else along * RING + i
                    pltpu.make_async_remote_copy(
                        src_ref=g_ref.at[row, source],
                        dst_ref=recv.at[side, i * RING + own, place],
                        send_sem=g_send,
                        recv_sem=g_recv.at[side, number],
                        device_id=(target, bf),
                        device_id_type=MESH,
                    ).start()
            for d in (2, 1, 3):
                along = (other + d) % RING
                target = along * RING + y if side == 0 else z * RING + along
                for k, (src, dst) in enumerate(moments):
                    pltpu.make_async_remote_copy(
                        src_ref=src.at[0, source],
                        dst_ref=dst.at[side, other, place],
                        send_sem=m_send.at[k],
                        recv_sem=m_recv.at[k, side, number],
                        device_id=(target, bf),
                        device_id_type=MESH,
                    ).start()
            for i in range(RING):
                row = i * RING + own if side == 0 else own * RING + i
                pltpu.make_async_copy(
                    g_ref.at[row, source], recv.at[side, i * RING + own, place], g_recv.at[side, number]
                ).start()
            for k, (src, dst) in enumerate(moments):
                pltpu.make_async_copy(
                    src.at[0, source], dst.at[side, other, place], m_recv.at[k, side, number]
                ).start()

    for number, (spans, first) in enumerate(order):
        send_chunk(number, spans, first)

    samples.wait()
    pools.wait()
    codes = jnp.concatenate([rows_ref[:, b * width : (b + 1) * width] for b in range(BF)], axis=0)
    bit = (codes >> 8) & 1
    before = lax.broadcasted_iota(jnp.int32, (LANES, LANES), 0) < lax.broadcasted_iota(jnp.int32, (LANES, LANES), 1)
    before = jnp.where(before, 1.0, 0.0).astype(jnp.bfloat16)
    ones = jnp.zeros((BF, 1), jnp.float32)
    ranks = []
    for b in range(width // LANES):
        piece = bit[:, b * LANES : (b + 1) * LANES].astype(jnp.float32)
        ranks.append(jnp.dot(piece.astype(jnp.bfloat16), before, preferred_element_type=jnp.float32) + ones)
        ones = ones + jnp.sum(piece, axis=1, keepdims=True)
    rank = jnp.concatenate(ranks, axis=1).astype(jnp.int32)
    zeros = width - ones.astype(jnp.int32)
    lane = lax.broadcasted_iota(jnp.int32, (BF, width), 1)
    slots[...] = jnp.where(bit == 1, TILE + zeros + rank, lane - rank)
    for b in range(BF):
        zero_count = width - jnp.sum(bit[b : b + 1])
        for u in range(slotted // TILE):
            which[b * (slotted // TILE) + u] = (u * TILE >= zero_count).astype(jnp.int32)

    def one_hot(slot):
        index = lax.broadcasted_iota(jnp.int32, (LANES, width), 0)
        return jnp.where(index == (slot & (LANES - 1)), 1.0, 0.0).astype(jnp.bfloat16)

    index = lax.broadcasted_iota(jnp.int32, (16, slotted), 0)
    member = lax.broadcasted_iota(jnp.int32, (8, slotted), 0)
    upper = member >= RING
    step_mask = jnp.where(upper, (z * RING * BF + bf) * block_len, (y * BF + bf) * block_len) + member * (GROUP * DEPTH)
    row_mask = jnp.where(upper, (member - RING) * BF, member * BF * RING) * block_len

    def signs(b, carry):
        code = rows_ref[:, pl.ds(pl.multiple_of(b * width, width), width)]
        slot = slots[pl.ds(b, 1), :]
        here = lax.broadcasted_iota(jnp.int32, (16, width), 0) == (slot >> 7)
        pieces = [jnp.where(here, (code >> shift) & 255, 0).astype(jnp.float32) for shift in (0, 8, 16)]
        pieces = jnp.concatenate(pieces, axis=0).astype(jnp.bfloat16)
        moved = lax.dot_general(
            pieces, one_hot(slot), (((1,), (1,)), ((), ())), preferred_element_type=jnp.float32
        ).astype(jnp.int32)
        moved = moved[0:16] + (moved[16:32] << 8) + (moved[32:48] << 16)
        rows = jnp.concatenate([moved[i : i + 1] for i in range(slotted // LANES)], axis=1)
        rows = jnp.broadcast_to(rows, (16, slotted))
        place = pl.ds(pl.multiple_of(b * slotted, slotted), slotted)
        fine = parity_sign(rows & index, 4)
        coarse[...] = parity_sign((rows >> 4) & index, 4)
        for i in range(16):
            weight[i * 16 : (i + 1) * 16, place] = (fine * coarse[i : i + 1, :]).astype(jnp.bfloat16)
        sign_low[:, place] = parity_sign((rows[:8] >> 9) & (index[:8] & 7), 4)
        sign_high[:, place] = parity_sign(rows[:8] & step_mask, 32)
        sign_row[:, place] = parity_sign((rows[:8] & row_mask) >> 18, 4)
        return carry

    lax.fori_loop(0, BF, signs, 0, unroll=2)
    unsort[...] = one_hot(slots[pl.ds(bf, 1), :])
    part[...] = jnp.zeros_like(part)

    above = lax.broadcasted_iota(jnp.int32, (8, DEPTH), 0) < RING

    def features(side, number, spans, first):
        size = spans * DEPTH
        place = pl.ds(pl.multiple_of(first * DEPTH, 4 * DEPTH), size)
        whole = recv.at[side, :, place]
        pltpu.make_async_copy(whole, whole, g_recv.at[side, number]).wait()
        for k, (_, dst) in enumerate(moments):
            whole = dst.at[side, :, place]
            pltpu.make_async_copy(whole, whole, m_recv.at[k, side, number]).wait()
        def feature(j):
            span = pl.ds(pl.multiple_of((first + j) * DEPTH, DEPTH), DEPTH)
            found = []
            for h in (0, 1):
                grad = recv[side, 8 * h : 8 * h + 8, span]

                def both(ref):
                    return jnp.where(above, ref[side, 2 * h : 2 * h + 1, span], ref[side, 2 * h + 1 : 2 * h + 2, span])

                moment_new = BETA_ONE * both(one) + (1.0 - BETA_ONE) * grad
                second_new = BETA_TWO * both(two) + (1.0 - BETA_TWO) * grad * grad
                found.append(both(flip).astype(jnp.float32) * moment_new * lax.rsqrt(second_new))
            return jnp.concatenate(found, axis=0)

        for q in range(spans // 2):
            even, odd = feature(2 * q), feature(2 * q + 1)
            for value, combined in ((0, even + odd), (1, even - odd)):
                top = combined.astype(jnp.bfloat16)
                rest = (combined - top.astype(jnp.float32)).astype(jnp.bfloat16)
                left[value, q * 16 : (q + 1) * 16, :] = top
                at = (spans // 2 + q) * 16
                left[value, at : at + 16, :] = rest

    def tile(side, spans, first, t):
        half = spans // 2
        found = []
        for u in range(slotted // TILE):
            place = pl.ds(pl.multiple_of(t * slotted + u * TILE, TILE), TILE)
            value = which[t * (slotted // TILE) + u]
            rows = left[value, : spans * 16, :]
            product = jnp.dot(rows, weight[:, place], preferred_element_type=jnp.float32)
            product = product[: half * 16] + product[half * 16 :]
            sign = sign_low[:, place]
            if spans < GROUP:
                sign = jnp.where(first % GROUP == 8, sign[4:8], sign[0:4])
            total = product[0:16] * sign[0:1]
            for j in range(1, half):
                total = total + product[j * 16 : (j + 1) * 16] * sign[j : j + 1]
            step_sign = sign_high[pl.ds(side * (side_len // (GROUP * DEPTH)) + first // GROUP, 1), place]
            found.append(part[side, :, place] + total * step_sign)
        return jnp.concatenate(found, axis=1)

    def do_chunk(side, number, spans, first):
        features(side, number, spans, first)
        for t in range(BF):
            part[side, :, t * slotted : (t + 1) * slotted] = tile(side, spans, first, t)

    def by_example(side, total, place):
        sign = sign_row[side * RING : (side + 1) * RING, place]
        found = total[0:RING] * sign[0:1]
        for i in range(1, RING):
            found = found + total[i * RING : (i + 1) * RING] * sign[i : i + 1]
        return found

    def bf_copy(side, slot):
        return pltpu.make_async_remote_copy(
            src_ref=outbox.at[side, slot],
            dst_ref=inbox.at[side, slot],
            send_sem=bf_send.at[side, slot],
            recv_sem=bf_recv.at[side, slot],
            device_id=(ex, bf_peer(*TILES[slot])),
            device_id_type=MESH,
        )

    number, start = 0, 0
    for spans, many in PLAN:

        def step_chunk(step, carry, spans=spans, number=number, start=start):
            do_chunk(step % 2, number + step // 2, spans, start + step // 2 * spans)
            return carry

        steps = 2 * many - (2 if number + many == len(order) else 0)
        lax.fori_loop(0, steps, step_chunk, 0)
        number, start = number + many, start + many * spans

    number, (spans, first) = len(order) - 1, order[-1]
    tiles = [bf_peer(*peer) for peer in TILES] + [bf]
    do_chunk(0, number, spans, first)
    for side in (0, 1):
        if side == 1:
            features(side, number, spans, first)
        for slot, t in enumerate(tiles):
            place = pl.ds(pl.multiple_of(t * slotted, slotted), slotted)
            total = part[side, :, place] if side == 0 else tile(side, spans, first, t)
            if slot < len(TILES):
                outbox[side, slot] = by_example(side, total, place)
                bf_copy(side, slot).start()
            else:
                inbox[side, slot] = by_example(side, total, place)
    summed = []
    for side in (0, 1):
        found = inbox[side, BF - 1]
        for slot in range(BF - 1):
            bf_copy(side, slot).wait_recv()
            found = found + inbox[side, slot]
        summed.append(found)

    found = jnp.concatenate(summed, axis=0)
    terms = []
    for _ in range(3):
        term = found.astype(jnp.bfloat16).astype(jnp.float32)
        found = found - term
        terms += [term[:, i * LANES : (i + 1) * LANES] for i in range(slotted // LANES)]
    stacked = jnp.concatenate(terms, axis=0).astype(jnp.bfloat16)
    spread = jnp.dot(stacked, unsort[...], preferred_element_type=jnp.float32)
    size = slotted // LANES * 8
    spread = spread[:size] + spread[size : 2 * size] + spread[2 * size :]
    chosen = jnp.broadcast_to(slots[pl.ds(bf, 1), :] >> 7, (8, width))
    summed = jnp.zeros((8, width), jnp.float32)
    for i in range(slotted // LANES):
        summed = summed + jnp.where(chosen == i, spread[8 * i : 8 * i + 8], 0.0)

    row = lax.broadcasted_iota(jnp.int32, (EX, width), 0)
    pooled = jnp.zeros((EX, width), jnp.float32)
    for i in range(RING):
        pooled = pooled + jnp.where(row == pool_ref[z * RING + i], summed[i : i + 1], 0.0)
        pooled = pooled + jnp.where(row == pool_ref[i * RING + y], summed[RING + i : RING + i + 1], 0.0)
    mine[...] = pooled
    for dz, dy in STEPS:
        target = owner(dz, dy)
        pltpu.make_async_remote_copy(
            src_ref=mine.at[target],
            dst_ref=got_ex.at[ex],
            send_sem=ex_send,
            recv_sem=ex_recv,
            device_id=(target, bf),
            device_id_type=MESH,
        ).start()
    pltpu.make_async_copy(mine.at[ex], got_ex.at[ex], ex_recv).start()
    for side in (0, 1):
        for slot in range(BF - 1):
            bf_copy(side, slot).wait_send()
    for part_rows in (8, 4):
        sent = g_ref.at[pl.ds(0, part_rows)]
        pltpu.make_async_copy(sent, sent, g_send).wait()
    for k, (src, _) in enumerate(moments):
        for _ in range(3):
            pltpu.make_async_copy(src, src, m_send.at[k]).wait()
    pltpu.make_async_copy(got_ex, got_ex, ex_recv).wait()
    scale = float(block_len * EX * BF) ** -0.5
    out_ref[...] = jnp.sum(got_ex[...], axis=0, keepdims=True) * scale
    for _ in STEPS:
        pltpu.make_async_copy(mine.at[0], mine.at[0], ex_send).wait()


def per_device(gradients, moment_one, moment_two, rademacher, sample_rows, pool_order):
    block_len = moment_one.shape[0]
    count = sample_rows.shape[0]
    side_len = block_len // 2
    width = count // BF
    slotted = width + TILE
    slot_count = slotted * BF
    chunks = len(list(chunk_list()))
    dma = pltpu.SemaphoreType.DMA
    return pl.pallas_call(
        kernel,
        out_shape=pltpu.VMEM((1, width), jnp.float32),
        in_specs=[pl.BlockSpec(memory_space=pl.ANY)] * 6,
        out_specs=pl.BlockSpec(memory_space=pltpu.VMEM),
        scratch_shapes=[
            pltpu.VMEM((1, count), jnp.int32),
            pltpu.SMEM((EX,), jnp.int32),
            pltpu.VMEM((2, EX, side_len), jnp.float32),
            pltpu.VMEM((2, RING, side_len), jnp.float32),
            pltpu.VMEM((2, RING, side_len), jnp.float32),
            pltpu.VMEM((2, RING, side_len), jnp.int32),
            pltpu.VMEM((DEPTH, slot_count), jnp.bfloat16),
            pltpu.VMEM((16, slotted), jnp.float32),
            pltpu.VMEM((GROUP // 2, slot_count), jnp.float32),
            pltpu.VMEM((block_len // (GROUP * DEPTH), slot_count), jnp.float32),
            pltpu.VMEM((2 * RING, slot_count), jnp.float32),
            pltpu.VMEM((2, GROUP * EX, DEPTH), jnp.bfloat16),
            pltpu.VMEM((BF, width), jnp.int32),
            pltpu.VMEM((LANES, width), jnp.bfloat16),
            pltpu.SMEM((slot_count // TILE,), jnp.int32),
            pltpu.VMEM((2, EX, slot_count), jnp.float32),
            pltpu.VMEM((2, BF - 1, RING, slotted), jnp.float32),
            pltpu.VMEM((2, BF, RING, slotted), jnp.float32),
            pltpu.VMEM((EX, width), jnp.float32),
            pltpu.VMEM((EX, width), jnp.float32),
            dma,
            dma((2, chunks)),
            dma((3,)),
            dma((3, 2, chunks)),
            dma((2, BF - 1)),
            dma((2, BF - 1)),
            dma,
            dma,
            dma((2,)),
        ],
        compiler_params=pltpu.CompilerParams(
            collective_id=0, has_side_effects=True, vmem_limit_bytes=56 * 2**20
        ),
    )(
        gradients.reshape(EX, block_len),
        moment_one.reshape(1, block_len),
        moment_two.reshape(1, block_len),
        rademacher.reshape(1, block_len),
        sample_rows.reshape(1, count),
        pool_order,
    )


def solution(mesh):
    in_specs = (P("ex", None, "bf"), P(("ex", "bf")), P(("ex", "bf")), P(("ex", "bf")), P(), P())
    out_specs = P("ex", "bf")
    return jax.shard_map(
        per_device, mesh=mesh, in_specs=in_specs, out_specs=out_specs, check_vma=False
    )
```

```python
import functools

import jax
import jax.numpy as jnp
from jax import lax
from jax.experimental import pallas as pl
from jax.experimental.pallas import tpu as pltpu
from jax.sharding import PartitionSpec as P

MESH = pl.DeviceIdType.MESH
BETA_ONE = 0.9
BETA_TWO = 0.999
RING = 4
EX = RING * RING
BF = 2 * RING
DEPTH = 256
GROUP = 16
PLAN = [(8, 2), (16, 2), (8, 2)]
LANES = 128
TILE = 256

STEPS = [(2, 2), (2, 1), (2, 3), (1, 2), (3, 2), (1, 1), (1, 3), (3, 1), (3, 3), (2, 0), (0, 2), (0, 1), (1, 0), (0, 3), (3, 0)]
TILES = [(2, 0), (2, 1), (1, 0), (1, 1), (3, 0), (3, 1), (0, 1)]


def parity_sign(values, bits):
    while bits > 1:
        bits = bits // 2
        values = values ^ (values >> bits)
    return (1 - 2 * (values & 1)).astype(jnp.float32)


def chunk_list():
    start = 0
    for spans, many in PLAN:
        for _ in range(many):
            yield spans, start
            start += spans


def kernel(
    g_ref, one_ref, two_ref, flip_ref, rows_hbm, pool_hbm, out_ref,
    rows_ref, pool_ref, recv, one, two, flip, weight, coarse, sign_low, sign_high, sign_row, left, slots, unsort, which, part, outbox, inbox, mine, got_ex,
    g_send, g_recv, m_send, m_recv, bf_send, bf_recv, ex_send, ex_recv, local_sem,
):
    ex = lax.axis_index("ex")
    bf = lax.axis_index("bf")
    z, y = ex // RING, ex % RING
    block_len = g_ref.shape[1]
    count = rows_hbm.shape[1]
    side_len = block_len // 2
    width = count // BF
    slotted = width + TILE
    order = list(chunk_list())

    def owner(dz, dy):
        return (z + dz) % RING * RING + (y + dy) % RING

    def bf_peer(dx, flip_core):
        core = bf % 2
        return (bf // 2 + dx) % RING * 2 + (1 - core if flip_core else core)

    samples = pltpu.make_async_copy(rows_hbm, rows_ref, local_sem.at[0])
    pools = pltpu.make_async_copy(pool_hbm, pool_ref, local_sem.at[1])

    barrier = pltpu.get_barrier_semaphore()
    for d in (2, 1, 3):
        pl.semaphore_signal(barrier, inc=1, device_id=(owner(d, 0), bf), device_id_type=MESH)
        pl.semaphore_signal(barrier, inc=1, device_id=(owner(0, d), bf), device_id_type=MESH)
    for dx, flip_core in TILES:
        pl.semaphore_signal(barrier, inc=1, device_id=(ex, bf_peer(dx, flip_core)), device_id_type=MESH)
    samples.start()
    pools.start()
    pl.semaphore_wait(barrier, 2 * (RING - 1) + BF - 1)

    moments = ((one_ref, one), (two_ref, two), (flip_ref, flip))

    def send_chunk(side, number, spans, first):
        size = spans * DEPTH
        for _ in (0,):
            own, other = (y, z) if side == 0 else (z, y)
            source = pl.ds(side * side_len + first * DEPTH, size)
            place = pl.ds(first * DEPTH, size)
            for d in (2, 1, 3):
                along = (own + d) % RING
                target = z * RING + along if side == 0 else along * RING + y
                for i in range(RING):
                    row = i * RING + along if side == 0 else along * RING + i
                    pltpu.make_async_remote_copy(
                        src_ref=g_ref.at[row, source],
                        dst_ref=recv.at[side, i * RING + own, place],
                        send_sem=g_send,
                        recv_sem=g_recv.at[side, number],
                        device_id=(target, bf),
                        device_id_type=MESH,
                    ).start()
            for d in (2, 1, 3):
                along = (other + d) % RING
                target = along * RING + y if side == 0 else z * RING + along
                for k, (src, dst) in enumerate(moments):
                    pltpu.make_async_remote_copy(
                        src_ref=src.at[0, source],
                        dst_ref=dst.at[side, other, place],
                        send_sem=m_send.at[k],
                        recv_sem=m_recv.at[k, side, number],
                        device_id=(target, bf),
                        device_id_type=MESH,
                    ).start()
            for i in range(RING):
                row = i * RING + own if side == 0 else own * RING + i
                pltpu.make_async_copy(
                    g_ref.at[row, source], recv.at[side, i * RING + own, place], g_recv.at[side, number]
                ).start()
            for k, (src, dst) in enumerate(moments):
                pltpu.make_async_copy(
                    src.at[0, source], dst.at[side, other, place], m_recv.at[k, side, number]
                ).start()

    for side, number in [(0,0),(1,0),(0,1),(1,1),(0,2),(1,2),(0,3),(1,3),(0,4),(0,5),(1,4),(1,5)]:
        send_chunk(side, number, *order[number])

    samples.wait()
    pools.wait()
    codes = jnp.concatenate([rows_ref[:, b * width : (b + 1) * width] for b in range(BF)], axis=0)
    bit = (codes >> 8) & 1
    before = lax.broadcasted_iota(jnp.int32, (LANES, LANES), 0) < lax.broadcasted_iota(jnp.int32, (LANES, LANES), 1)
    before = jnp.where(before, 1.0, 0.0).astype(jnp.bfloat16)
    ones = jnp.zeros((BF, 1), jnp.float32)
    ranks = []
    for b in range(width // LANES):
        piece = bit[:, b * LANES : (b + 1) * LANES].astype(jnp.float32)
        ranks.append(jnp.dot(piece.astype(jnp.bfloat16), before, preferred_element_type=jnp.float32) + ones)
        ones = ones + jnp.sum(piece, axis=1, keepdims=True)
    rank = jnp.concatenate(ranks, axis=1).astype(jnp.int32)
    zeros = width - ones.astype(jnp.int32)
    lane = lax.broadcasted_iota(jnp.int32, (BF, width), 1)
    slots[...] = jnp.where(bit == 1, TILE + zeros + rank, lane - rank)
    for b in range(BF):
        zero_count = width - jnp.sum(bit[b : b + 1])
        for u in range(slotted // TILE):
            which[b * (slotted // TILE) + u] = (u * TILE >= zero_count).astype(jnp.int32)

    def one_hot(slot):
        index = lax.broadcasted_iota(jnp.int32, (LANES, width), 0)
        return jnp.where(index == (slot & (LANES - 1)), 1.0, 0.0).astype(jnp.bfloat16)

    index = lax.broadcasted_iota(jnp.int32, (16, slotted), 0)
    member = lax.broadcasted_iota(jnp.int32, (8, slotted), 0)
    upper = member >= RING
    step_mask = jnp.where(upper, (z * RING * BF + bf) * block_len, (y * BF + bf) * block_len) + member * (GROUP * DEPTH)
    row_mask = jnp.where(upper, (member - RING) * BF, member * BF * RING) * block_len

    def signs(b, carry):
        code = rows_ref[:, pl.ds(pl.multiple_of(b * width, width), width)]
        slot = slots[pl.ds(b, 1), :]
        here = lax.broadcasted_iota(jnp.int32, (16, width), 0) == (slot >> 7)
        pieces = [jnp.where(here, (code >> shift) & 255, 0).astype(jnp.float32) for shift in (0, 8, 16)]
        pieces = jnp.concatenate(pieces, axis=0).astype(jnp.bfloat16)
        moved = lax.dot_general(
            pieces, one_hot(slot), (((1,), (1,)), ((), ())), preferred_element_type=jnp.float32
        ).astype(jnp.int32)
        moved = moved[0:16] + (moved[16:32] << 8) + (moved[32:48] << 16)
        rows = jnp.concatenate([moved[i : i + 1] for i in range(slotted // LANES)], axis=1)
        rows = jnp.broadcast_to(rows, (16, slotted))
        place = pl.ds(pl.multiple_of(b * slotted, slotted), slotted)
        fine = parity_sign(rows & index, 4)
        coarse[...] = parity_sign((rows >> 4) & index, 4)
        for i in range(16):
            weight[i * 16 : (i + 1) * 16, place] = (fine * coarse[i : i + 1, :]).astype(jnp.bfloat16)
        sign_low[:, place] = parity_sign((rows[:8] >> 9) & (index[:8] & 7), 4)
        sign_high[:, place] = parity_sign(rows[:8] & step_mask, 32)
        sign_row[:, place] = parity_sign((rows[:8] & row_mask) >> 18, 4)
        return carry

    lax.fori_loop(0, BF, signs, 0, unroll=8)
    unsort[...] = one_hot(slots[pl.ds(bf, 1), :])
    part[...] = jnp.zeros_like(part)

    above = lax.broadcasted_iota(jnp.int32, (8, DEPTH), 0) < RING

    def features(side, number, spans, first):
        size = spans * DEPTH
        place = pl.ds(pl.multiple_of(first * DEPTH, 4 * DEPTH), size)
        whole = recv.at[side, :, place]
        pltpu.make_async_copy(whole, whole, g_recv.at[side, number]).wait()
        for k, (_, dst) in enumerate(moments):
            whole = dst.at[side, :, place]
            pltpu.make_async_copy(whole, whole, m_recv.at[k, side, number]).wait()
        def feature(j):
            span = pl.ds(pl.multiple_of((first + j) * DEPTH, DEPTH), DEPTH)
            found = []
            for h in (0, 1):
                grad = recv[side, 8 * h : 8 * h + 8, span]

                def both(ref):
                    return jnp.where(above, ref[side, 2 * h : 2 * h + 1, span], ref[side, 2 * h + 1 : 2 * h + 2, span])

                moment_new = BETA_ONE * both(one) + (1.0 - BETA_ONE) * grad
                second_new = BETA_TWO * both(two) + (1.0 - BETA_TWO) * grad * grad
                found.append(both(flip).astype(jnp.float32) * moment_new * lax.rsqrt(second_new))
            return jnp.concatenate(found, axis=0)

        for q in range(spans // 2):
            even, odd = feature(2 * q), feature(2 * q + 1)
            for value, combined in ((0, even + odd), (1, even - odd)):
                top = combined.astype(jnp.bfloat16)
                rest = (combined - top.astype(jnp.float32)).astype(jnp.bfloat16)
                left[value, q * 16 : (q + 1) * 16, :] = top
                at = (spans // 2 + q) * 16
                left[value, at : at + 16, :] = rest

    def tile(side, spans, first, t):
        half = spans // 2
        found = []
        for u in range(slotted // TILE):
            place = pl.ds(pl.multiple_of(t * slotted + u * TILE, TILE), TILE)
            value = which[t * (slotted // TILE) + u]
            rows = left[value, : spans * 16, :]
            product = jnp.dot(rows, weight[:, place], preferred_element_type=jnp.float32)
            product = product[: half * 16] + product[half * 16 :]
            sign = sign_low[:, place]
            if spans < GROUP:
                sign = jnp.where(first % GROUP == 8, sign[4:8], sign[0:4])
            total = product[0:16] * sign[0:1]
            for j in range(1, half):
                total = total + product[j * 16 : (j + 1) * 16] * sign[j : j + 1]
            step_sign = sign_high[pl.ds(side * (side_len // (GROUP * DEPTH)) + first // GROUP, 1), place]
            found.append(part[side, :, place] + total * step_sign)
        return jnp.concatenate(found, axis=1)

    def do_chunk(side, number, spans, first):
        features(side, number, spans, first)
        for t in range(BF):
            part[side, :, t * slotted : (t + 1) * slotted] = tile(side, spans, first, t)

    def by_example(side, total, place):
        sign = sign_row[side * RING : (side + 1) * RING, place]
        found = total[0:RING] * sign[0:1]
        for i in range(1, RING):
            found = found + total[i * RING : (i + 1) * RING] * sign[i : i + 1]
        return found

    def bf_copy(side, slot):
        return pltpu.make_async_remote_copy(
            src_ref=outbox.at[side, slot],
            dst_ref=inbox.at[side, slot],
            send_sem=bf_send.at[side, slot],
            recv_sem=bf_recv.at[side, slot],
            device_id=(ex, bf_peer(*TILES[slot])),
            device_id_type=MESH,
        )

    number, start = 0, 0
    for spans, many in PLAN[:2]:

        def step_chunk(step, carry, spans=spans, number=number, start=start):
            do_chunk(step % 2, number + step // 2, spans, start + step // 2 * spans)
            return carry

        lax.fori_loop(0, 2 * many, step_chunk, 0)
        number, start = number + many, start + many * spans

    spans, many = PLAN[2]

    def step_side(step, carry):
        do_chunk(0, number + step, spans, start + step * spans)
        return carry

    lax.fori_loop(0, many, step_side, 0)
    number, (spans, first) = len(order) - 1, order[-1]
    tiles = [bf_peer(*peer) for peer in TILES] + [bf]
    for side in (0, 1):
        if side == 1:
            do_chunk(side, number - 1, *order[number - 1])
            features(side, number, spans, first)
        size = BF if side == 0 else 2
        for begin in range(0, BF, size):
            for slot in range(begin, begin + size):
                place = pl.ds(pl.multiple_of(tiles[slot] * slotted, slotted), slotted)
                total = part[side, :, place] if side == 0 else tile(side, spans, first, tiles[slot])
                if slot < len(TILES):
                    outbox[side, slot] = by_example(side, total, place)
                else:
                    inbox[side, slot] = by_example(side, total, place)
            for slot in range(begin, min(begin + size, len(TILES))):
                bf_copy(side, slot).start()
    summed = []
    for side in (0, 1):
        found = inbox[side, BF - 1]
        for slot in range(BF - 1):
            bf_copy(side, slot).wait_recv()
            found = found + inbox[side, slot]
        summed.append(found)

    found = jnp.concatenate(summed, axis=0)
    terms = []
    for _ in range(3):
        term = found.astype(jnp.bfloat16).astype(jnp.float32)
        found = found - term
        terms += [term[:, i * LANES : (i + 1) * LANES] for i in range(slotted // LANES)]
    stacked = jnp.concatenate(terms, axis=0).astype(jnp.bfloat16)
    spread = jnp.dot(stacked, unsort[...], preferred_element_type=jnp.float32)
    size = slotted // LANES * 8
    spread = spread[:size] + spread[size : 2 * size] + spread[2 * size :]
    chosen = jnp.broadcast_to(slots[pl.ds(bf, 1), :] >> 7, (8, width))
    summed = jnp.zeros((8, width), jnp.float32)
    for i in range(slotted // LANES):
        summed = summed + jnp.where(chosen == i, spread[8 * i : 8 * i + 8], 0.0)

    row = lax.broadcasted_iota(jnp.int32, (EX, width), 0)
    pooled = jnp.zeros((EX, width), jnp.float32)
    for i in range(RING):
        pooled = pooled + jnp.where(row == pool_ref[z * RING + i], summed[i : i + 1], 0.0)
        pooled = pooled + jnp.where(row == pool_ref[i * RING + y], summed[RING + i : RING + i + 1], 0.0)
    mine[...] = pooled
    for dz, dy in STEPS:
        target = owner(dz, dy)
        pltpu.make_async_remote_copy(
            src_ref=mine.at[target],
            dst_ref=got_ex.at[ex],
            send_sem=ex_send,
            recv_sem=ex_recv,
            device_id=(target, bf),
            device_id_type=MESH,
        ).start()
    pltpu.make_async_copy(mine.at[ex], got_ex.at[ex], ex_recv).start()
    for side in (0, 1):
        for slot in range(BF - 1):
            bf_copy(side, slot).wait_send()
    for part_rows in (8, 4):
        sent = g_ref.at[pl.ds(0, part_rows)]
        pltpu.make_async_copy(sent, sent, g_send).wait()
    for k, (src, _) in enumerate(moments):
        for _ in range(3):
            pltpu.make_async_copy(src, src, m_send.at[k]).wait()
    pltpu.make_async_copy(got_ex, got_ex, ex_recv).wait()
    scale = float(block_len * EX * BF) ** -0.5
    out_ref[...] = jnp.sum(got_ex[...], axis=0, keepdims=True) * scale
    for _ in STEPS:
        pltpu.make_async_copy(mine.at[0], mine.at[0], ex_send).wait()


def per_device(gradients, moment_one, moment_two, rademacher, sample_rows, pool_order):
    block_len = moment_one.shape[0]
    count = sample_rows.shape[0]
    side_len = block_len // 2
    width = count // BF
    slotted = width + TILE
    slot_count = slotted * BF
    chunks = len(list(chunk_list()))
    dma = pltpu.SemaphoreType.DMA
    return pl.pallas_call(
        kernel,
        out_shape=pltpu.VMEM((1, width), jnp.float32),
        in_specs=[pl.BlockSpec(memory_space=pl.ANY)] * 6,
        out_specs=pl.BlockSpec(memory_space=pltpu.VMEM),
        scratch_shapes=[
            pltpu.VMEM((1, count), jnp.int32),
            pltpu.SMEM((EX,), jnp.int32),
            pltpu.VMEM((2, EX, side_len), jnp.float32),
            pltpu.VMEM((2, RING, side_len), jnp.float32),
            pltpu.VMEM((2, RING, side_len), jnp.float32),
            pltpu.VMEM((2, RING, side_len), jnp.int32),
            pltpu.VMEM((DEPTH, slot_count), jnp.bfloat16),
            pltpu.VMEM((16, slotted), jnp.float32),
            pltpu.VMEM((GROUP // 2, slot_count), jnp.float32),
            pltpu.VMEM((block_len // (GROUP * DEPTH), slot_count), jnp.float32),
            pltpu.VMEM((2 * RING, slot_count), jnp.float32),
            pltpu.VMEM((2, GROUP * EX, DEPTH), jnp.bfloat16),
            pltpu.VMEM((BF, width), jnp.int32),
            pltpu.VMEM((LANES, width), jnp.bfloat16),
            pltpu.SMEM((slot_count // TILE,), jnp.int32),
            pltpu.VMEM((2, EX, slot_count), jnp.float32),
            pltpu.VMEM((2, BF - 1, RING, slotted), jnp.float32),
            pltpu.VMEM((2, BF, RING, slotted), jnp.float32),
            pltpu.VMEM((EX, width), jnp.float32),
            pltpu.VMEM((EX, width), jnp.float32),
            dma,
            dma((2, chunks)),
            dma((3,)),
            dma((3, 2, chunks)),
            dma((2, BF - 1)),
            dma((2, BF - 1)),
            dma,
            dma,
            dma((2,)),
        ],
        compiler_params=pltpu.CompilerParams(
            collective_id=0, has_side_effects=True, vmem_limit_bytes=56 * 2**20
        ),
    )(
        gradients.reshape(EX, block_len),
        moment_one.reshape(1, block_len),
        moment_two.reshape(1, block_len),
        rademacher.reshape(1, block_len),
        sample_rows.reshape(1, count),
        pool_order,
    )


def solution(mesh):
    in_specs = (P("ex", None, "bf"), P(("ex", "bf")), P(("ex", "bf")), P(("ex", "bf")), P(), P())
    out_specs = P("ex", "bf")
    return jax.shard_map(
        per_device, mesh=mesh, in_specs=in_specs, out_specs=out_specs, check_vma=False
    )
```

```python
import functools

import jax
import jax.numpy as jnp
from jax import lax
from jax.experimental import pallas as pl
from jax.experimental.pallas import tpu as pltpu
from jax.sharding import PartitionSpec as P

MESH = pl.DeviceIdType.MESH
BETA_ONE = 0.9
BETA_TWO = 0.999
RING = 4
EX = RING * RING
BF = 2 * RING
DEPTH = 256
GROUP = 16
PLAN = [(8, 2), (16, 2), (8, 2)]
LANES = 128
TILE = 256

STEPS = [(2, 2), (2, 1), (2, 3), (1, 2), (3, 2), (1, 1), (1, 3), (3, 1), (3, 3), (2, 0), (0, 2), (0, 1), (1, 0), (0, 3), (3, 0)]
TILES = [(2, 0), (2, 1), (1, 0), (1, 1), (3, 0), (3, 1), (0, 1)]


def parity_sign(values, bits):
    while bits > 1:
        bits = bits // 2
        values = values ^ (values >> bits)
    return (1 - 2 * (values & 1)).astype(jnp.float32)


def chunk_list():
    start = 0
    for spans, many in PLAN:
        for _ in range(many):
            yield spans, start
            start += spans


def kernel(
    g_ref, one_ref, two_ref, flip_ref, rows_hbm, pool_hbm, out_ref,
    rows_ref, pool_ref, recv, one, two, flip, weight, coarse, sign_low, sign_high, sign_row, left, slots, unsort, which, part, outbox, inbox, mine, got_ex,
    g_send, g_recv, m_send, m_recv, bf_send, bf_recv, ex_send, ex_recv, local_sem,
):
    ex = lax.axis_index("ex")
    bf = lax.axis_index("bf")
    z, y = ex // RING, ex % RING
    block_len = g_ref.shape[1]
    count = rows_hbm.shape[1]
    side_len = block_len // 2
    width = count // BF
    slotted = width + TILE
    order = list(chunk_list())

    def owner(dz, dy):
        return (z + dz) % RING * RING + (y + dy) % RING

    def bf_peer(dx, flip_core):
        core = bf % 2
        return (bf // 2 + dx) % RING * 2 + (1 - core if flip_core else core)

    samples = pltpu.make_async_copy(rows_hbm, rows_ref, local_sem.at[0])
    pools = pltpu.make_async_copy(pool_hbm, pool_ref, local_sem.at[1])

    barrier = pltpu.get_barrier_semaphore()
    for d in (2, 1, 3):
        pl.semaphore_signal(barrier, inc=1, device_id=(owner(d, 0), bf), device_id_type=MESH)
        pl.semaphore_signal(barrier, inc=1, device_id=(owner(0, d), bf), device_id_type=MESH)
    for dx, flip_core in TILES:
        pl.semaphore_signal(barrier, inc=1, device_id=(ex, bf_peer(dx, flip_core)), device_id_type=MESH)
    samples.start()
    pools.start()
    pl.semaphore_wait(barrier, 2 * (RING - 1) + BF - 1)

    moments = ((one_ref, one), (two_ref, two), (flip_ref, flip))

    def send_chunk(side, number, spans, first):
        size = spans * DEPTH
        for _ in (0,):
            own, other = (y, z) if side == 0 else (z, y)
            source = pl.ds(side * side_len + first * DEPTH, size)
            place = pl.ds(first * DEPTH, size)
            for d in (2, 1, 3):
                along = (own + d) % RING
                target = z * RING + along if side == 0 else along * RING + y
                for i in range(RING):
                    row = i * RING + along if side == 0 else along * RING + i
                    pltpu.make_async_remote_copy(
                        src_ref=g_ref.at[row, source],
                        dst_ref=recv.at[side, i * RING + own, place],
                        send_sem=g_send,
                        recv_sem=g_recv.at[side, number],
                        device_id=(target, bf),
                        device_id_type=MESH,
                    ).start()
            for d in (2, 1, 3):
                along = (other + d) % RING
                target = along * RING + y if side == 0 else z * RING + along
                for k, (src, dst) in enumerate(moments):
                    pltpu.make_async_remote_copy(
                        src_ref=src.at[0, source],
                        dst_ref=dst.at[side, other, place],
                        send_sem=m_send.at[k],
                        recv_sem=m_recv.at[k, side, number],
                        device_id=(target, bf),
                        device_id_type=MESH,
                    ).start()
            for i in range(RING):
                row = i * RING + own if side == 0 else own * RING + i
                pltpu.make_async_copy(
                    g_ref.at[row, source], recv.at[side, i * RING + own, place], g_recv.at[side, number]
                ).start()
            for k, (src, dst) in enumerate(moments):
                pltpu.make_async_copy(
                    src.at[0, source], dst.at[side, other, place], m_recv.at[k, side, number]
                ).start()

    for side, number in [(0,0),(1,0),(0,1),(1,1),(0,2),(1,2),(0,3),(1,3),(0,4),(0,5),(1,4),(1,5)]:
        send_chunk(side, number, *order[number])

    samples.wait()
    pools.wait()
    codes = jnp.concatenate([rows_ref[:, b * width : (b + 1) * width] for b in range(BF)], axis=0)
    bit = (codes >> 8) & 1
    before = lax.broadcasted_iota(jnp.int32, (LANES, LANES), 0) < lax.broadcasted_iota(jnp.int32, (LANES, LANES), 1)
    before = jnp.where(before, 1.0, 0.0).astype(jnp.bfloat16)
    ones = jnp.zeros((BF, 1), jnp.float32)
    ranks = []
    for b in range(width // LANES):
        piece = bit[:, b * LANES : (b + 1) * LANES].astype(jnp.float32)
        ranks.append(jnp.dot(piece.astype(jnp.bfloat16), before, preferred_element_type=jnp.float32) + ones)
        ones = ones + jnp.sum(piece, axis=1, keepdims=True)
    rank = jnp.concatenate(ranks, axis=1).astype(jnp.int32)
    zeros = width - ones.astype(jnp.int32)
    lane = lax.broadcasted_iota(jnp.int32, (BF, width), 1)
    slots[...] = jnp.where(bit == 1, TILE + zeros + rank, lane - rank)
    for b in range(BF):
        zero_count = width - jnp.sum(bit[b : b + 1])
        for u in range(slotted // TILE):
            which[b * (slotted // TILE) + u] = (u * TILE >= zero_count).astype(jnp.int32)

    def one_hot(slot):
        index = lax.broadcasted_iota(jnp.int32, (LANES, width), 0)
        return jnp.where(index == (slot & (LANES - 1)), 1.0, 0.0).astype(jnp.bfloat16)

    index = lax.broadcasted_iota(jnp.int32, (16, slotted), 0)
    member = lax.broadcasted_iota(jnp.int32, (8, slotted), 0)
    upper = member >= RING
    step_mask = jnp.where(upper, (z * RING * BF + bf) * block_len, (y * BF + bf) * block_len) + member * (GROUP * DEPTH)
    row_mask = jnp.where(upper, (member - RING) * BF, member * BF * RING) * block_len

    def signs(b, carry):
        code = rows_ref[:, pl.ds(pl.multiple_of(b * width, width), width)]
        slot = slots[pl.ds(b, 1), :]
        here = lax.broadcasted_iota(jnp.int32, (16, width), 0) == (slot >> 7)
        pieces = [jnp.where(here, (code >> shift) & 255, 0).astype(jnp.float32) for shift in (0, 8, 16)]
        pieces = jnp.concatenate(pieces, axis=0).astype(jnp.bfloat16)
        moved = lax.dot_general(
            pieces, one_hot(slot), (((1,), (1,)), ((), ())), preferred_element_type=jnp.float32
        ).astype(jnp.int32)
        moved = moved[0:16] + (moved[16:32] << 8) + (moved[32:48] << 16)
        rows = jnp.concatenate([moved[i : i + 1] for i in range(slotted // LANES)], axis=1)
        rows = jnp.broadcast_to(rows, (16, slotted))
        place = pl.ds(pl.multiple_of(b * slotted, slotted), slotted)
        fine = parity_sign(rows & index, 4)
        coarse[...] = parity_sign((rows >> 4) & index, 4)
        for i in range(16):
            weight[i * 16 : (i + 1) * 16, place] = (fine * coarse[i : i + 1, :]).astype(jnp.bfloat16)
        sign_low[:, place] = parity_sign((rows[:8] >> 9) & (index[:8] & 7), 4)
        sign_high[:, place] = parity_sign(rows[:8] & step_mask, 32)
        sign_row[:, place] = parity_sign((rows[:8] & row_mask) >> 18, 4)
        return carry

    lax.fori_loop(0, BF, signs, 0, unroll=8)
    unsort[...] = one_hot(slots[pl.ds(bf, 1), :])
    part[...] = jnp.zeros_like(part)

    above = lax.broadcasted_iota(jnp.int32, (8, DEPTH), 0) < RING

    def features(side, number, spans, first):
        size = spans * DEPTH
        place = pl.ds(pl.multiple_of(first * DEPTH, 4 * DEPTH), size)
        whole = recv.at[side, :, place]
        pltpu.make_async_copy(whole, whole, g_recv.at[side, number]).wait()
        for k, (_, dst) in enumerate(moments):
            whole = dst.at[side, :, place]
            pltpu.make_async_copy(whole, whole, m_recv.at[k, side, number]).wait()
        def feature(j):
            span = pl.ds(pl.multiple_of((first + j) * DEPTH, DEPTH), DEPTH)
            found = []
            for h in (0, 1):
                grad = recv[side, 8 * h : 8 * h + 8, span]

                def both(ref):
                    return jnp.where(above, ref[side, 2 * h : 2 * h + 1, span], ref[side, 2 * h + 1 : 2 * h + 2, span])

                moment_new = BETA_ONE * both(one) + (1.0 - BETA_ONE) * grad
                second_new = BETA_TWO * both(two) + (1.0 - BETA_TWO) * grad * grad
                found.append(both(flip).astype(jnp.float32) * moment_new * lax.rsqrt(second_new))
            return jnp.concatenate(found, axis=0)

        for q in range(spans // 2):
            even, odd = feature(2 * q), feature(2 * q + 1)
            for value, combined in ((0, even + odd), (1, even - odd)):
                top = combined.astype(jnp.bfloat16)
                rest = (combined - top.astype(jnp.float32)).astype(jnp.bfloat16)
                left[value, q * 16 : (q + 1) * 16, :] = top
                at = (spans // 2 + q) * 16
                left[value, at : at + 16, :] = rest

    def tile(side, spans, first, t):
        half = spans // 2
        found = []
        for u in range(slotted // TILE):
            place = pl.ds(pl.multiple_of(t * slotted + u * TILE, TILE), TILE)
            value = which[t * (slotted // TILE) + u]
            rows = left[value, : spans * 16, :]
            product = jnp.dot(rows, weight[:, place], preferred_element_type=jnp.float32)
            product = product[: half * 16] + product[half * 16 :]
            sign = sign_low[:, place]
            if spans < GROUP:
                sign = jnp.where(first % GROUP == 8, sign[4:8], sign[0:4])
            total = product[0:16] * sign[0:1]
            for j in range(1, half):
                total = total + product[j * 16 : (j + 1) * 16] * sign[j : j + 1]
            step_sign = sign_high[pl.ds(side * (side_len // (GROUP * DEPTH)) + first // GROUP, 1), place]
            found.append(part[side, :, place] + total * step_sign)
        return jnp.concatenate(found, axis=1)

    def do_chunk(side, number, spans, first):
        features(side, number, spans, first)
        for t in range(BF):
            part[side, :, t * slotted : (t + 1) * slotted] = tile(side, spans, first, t)

    def by_example(side, total, place):
        sign = sign_row[side * RING : (side + 1) * RING, place]
        found = total[0:RING] * sign[0:1]
        for i in range(1, RING):
            found = found + total[i * RING : (i + 1) * RING] * sign[i : i + 1]
        return found

    def bf_copy(side, slot):
        return pltpu.make_async_remote_copy(
            src_ref=outbox.at[side, slot],
            dst_ref=inbox.at[side, slot],
            send_sem=bf_send.at[side, slot],
            recv_sem=bf_recv.at[side, slot],
            device_id=(ex, bf_peer(*TILES[slot])),
            device_id_type=MESH,
        )

    number, start = 0, 0
    for spans, many in PLAN[:2]:

        def step_chunk(step, carry, spans=spans, number=number, start=start):
            do_chunk(step % 2, number + step // 2, spans, start + step // 2 * spans)
            return carry

        lax.fori_loop(0, 2 * many, step_chunk, 0)
        number, start = number + many, start + many * spans

    spans, many = PLAN[2]

    def step_side(step, carry):
        do_chunk(0, number + step, spans, start + step * spans)
        return carry

    lax.fori_loop(0, many, step_side, 0)
    number, (spans, first) = len(order) - 1, order[-1]
    tiles = [bf_peer(*peer) for peer in TILES] + [bf]
    for side in (0, 1):
        if side == 1:
            do_chunk(side, number - 1, *order[number - 1])
            features(side, number, spans, first)
        size = BF if side == 0 else 2
        for begin in range(0, BF, size):
            for slot in range(begin, begin + size):
                place = pl.ds(pl.multiple_of(tiles[slot] * slotted, slotted), slotted)
                total = part[side, :, place] if side == 0 else tile(side, spans, first, tiles[slot])
                if slot < len(TILES):
                    outbox[side, slot] = by_example(side, total, place)
                else:
                    inbox[side, slot] = by_example(side, total, place)
            for slot in range(begin, min(begin + size, len(TILES))):
                bf_copy(side, slot).start()
    summed = []
    for side in (0, 1):
        found = inbox[side, BF - 1]
        for slot in range(BF - 1):
            bf_copy(side, slot).wait_recv()
            found = found + inbox[side, slot]
        summed.append(found)

    found = jnp.concatenate(summed, axis=0)
    terms = []
    for _ in range(2):
        term = found.astype(jnp.bfloat16).astype(jnp.float32)
        found = found - term
        terms += [term[:, i * LANES : (i + 1) * LANES] for i in range(slotted // LANES)]
    stacked = jnp.concatenate(terms, axis=0).astype(jnp.bfloat16)
    spread = jnp.dot(stacked, unsort[...], preferred_element_type=jnp.float32)
    size = slotted // LANES * 8
    spread = spread[:size] + spread[size:]
    chosen = jnp.broadcast_to(slots[pl.ds(bf, 1), :] >> 7, (8, width))
    summed = jnp.zeros((8, width), jnp.float32)
    for i in range(slotted // LANES):
        summed = summed + jnp.where(chosen == i, spread[8 * i : 8 * i + 8], 0.0)

    row = lax.broadcasted_iota(jnp.int32, (EX, width), 0)
    pooled = jnp.zeros((EX, width), jnp.float32)
    for i in range(RING):
        pooled = pooled + jnp.where(row == pool_ref[z * RING + i], summed[i : i + 1], 0.0)
        pooled = pooled + jnp.where(row == pool_ref[i * RING + y], summed[RING + i : RING + i + 1], 0.0)
    mine[...] = pooled
    for dz, dy in STEPS:
        target = owner(dz, dy)
        pltpu.make_async_remote_copy(
            src_ref=mine.at[target],
            dst_ref=got_ex.at[ex],
            send_sem=ex_send,
            recv_sem=ex_recv,
            device_id=(target, bf),
            device_id_type=MESH,
        ).start()
    pltpu.make_async_copy(mine.at[ex], got_ex.at[ex], ex_recv).start()
    for side in (0, 1):
        for slot in range(BF - 1):
            bf_copy(side, slot).wait_send()
    for part_rows in (8, 4):
        sent = g_ref.at[pl.ds(0, part_rows)]
        pltpu.make_async_copy(sent, sent, g_send).wait()
    for k, (src, _) in enumerate(moments):
        for _ in range(3):
            pltpu.make_async_copy(src, src, m_send.at[k]).wait()
    pltpu.make_async_copy(got_ex, got_ex, ex_recv).wait()
    scale = float(block_len * EX * BF) ** -0.5
    out_ref[...] = jnp.sum(got_ex[...], axis=0, keepdims=True) * scale
    for _ in STEPS:
        pltpu.make_async_copy(mine.at[0], mine.at[0], ex_send).wait()


def per_device(gradients, moment_one, moment_two, rademacher, sample_rows, pool_order):
    block_len = moment_one.shape[0]
    count = sample_rows.shape[0]
    side_len = block_len // 2
    width = count // BF
    slotted = width + TILE
    slot_count = slotted * BF
    chunks = len(list(chunk_list()))
    dma = pltpu.SemaphoreType.DMA
    return pl.pallas_call(
        kernel,
        out_shape=pltpu.VMEM((1, width), jnp.float32),
        in_specs=[pl.BlockSpec(memory_space=pl.ANY)] * 6,
        out_specs=pl.BlockSpec(memory_space=pltpu.VMEM),
        scratch_shapes=[
            pltpu.VMEM((1, count), jnp.int32),
            pltpu.SMEM((EX,), jnp.int32),
            pltpu.VMEM((2, EX, side_len), jnp.float32),
            pltpu.VMEM((2, RING, side_len), jnp.float32),
            pltpu.VMEM((2, RING, side_len), jnp.float32),
            pltpu.VMEM((2, RING, side_len), jnp.int32),
            pltpu.VMEM((DEPTH, slot_count), jnp.bfloat16),
            pltpu.VMEM((16, slotted), jnp.float32),
            pltpu.VMEM((GROUP // 2, slot_count), jnp.float32),
            pltpu.VMEM((block_len // (GROUP * DEPTH), slot_count), jnp.float32),
            pltpu.VMEM((2 * RING, slot_count), jnp.float32),
            pltpu.VMEM((2, GROUP * EX, DEPTH), jnp.bfloat16),
            pltpu.VMEM((BF, width), jnp.int32),
            pltpu.VMEM((LANES, width), jnp.bfloat16),
            pltpu.SMEM((slot_count // TILE,), jnp.int32),
            pltpu.VMEM((2, EX, slot_count), jnp.float32),
            pltpu.VMEM((2, BF - 1, RING, slotted), jnp.float32),
            pltpu.VMEM((2, BF, RING, slotted), jnp.float32),
            pltpu.VMEM((EX, width), jnp.float32),
            pltpu.VMEM((EX, width), jnp.float32),
            dma,
            dma((2, chunks)),
            dma((3,)),
            dma((3, 2, chunks)),
            dma((2, BF - 1)),
            dma((2, BF - 1)),
            dma,
            dma,
            dma((2,)),
        ],
        compiler_params=pltpu.CompilerParams(
            collective_id=0, has_side_effects=True, vmem_limit_bytes=56 * 2**20
        ),
    )(
        gradients.reshape(EX, block_len),
        moment_one.reshape(1, block_len),
        moment_two.reshape(1, block_len),
        rademacher.reshape(1, block_len),
        sample_rows.reshape(1, count),
        pool_order,
    )


def solution(mesh):
    in_specs = (P("ex", None, "bf"), P(("ex", "bf")), P(("ex", "bf")), P(("ex", "bf")), P(), P())
    out_specs = P("ex", "bf")
    return jax.shard_map(
        per_device, mesh=mesh, in_specs=in_specs, out_specs=out_specs, check_vma=False
    )
```
